256 devices in a mesh: section: 2 (over core), beam: 32 (over z, x), tensor: 4 (over y).
Axes of the slice: x: 4, y: 4, z: 8, core: 2. Of those that a mesh axis runs over, the one named last changes fastest.
Arguments:
- streams_in: bfloat16 [64, 64, 8192], P('beam', None, 'tensor'), may hold values from -14 to 14
- beam_state_cache: bfloat16 [2, 64, 128, 64, 128], P('section', 'beam', 'tensor'), may hold values from -6 to 6
- conv_x_cache: bfloat16 [2, 64, 3, 8192], P('section', 'beam', None, 'tensor'), may hold values from -6 to 6
- conv_bc_cache: bfloat16 [2, 64, 3, 2, 1024], P('section', 'beam', None, None, 'tensor'), may hold values from -6 to 6
- bc_inputs: bfloat16 [2, 64, 64, 2, 1024], P('section', 'beam', None, None, 'tensor'), may hold values from -6 to 6
- unbiased_increments: float32 [2, 64, 64, 128], P('section', 'beam', None, 'tensor'), may hold values from -3 to 15
- parents: int32 [64], replicated, may hold values from 0 to 63, as said below
- lengths: int32 [64], P('beam'), may hold values from 1 to 64, as said below
- input_norm_gain: float32 [2, 8192], P('section', 'tensor'), may hold values from 0.1 to 1.9
- conv_x_weight: float32 [2, 4, 8192], P('section', None, 'tensor'), may hold values from -3 to 3
- conv_bc_weight: float32 [2, 4, 2, 1024], P('section', None, None, 'tensor'), may hold values from -3 to 3
- a_log: float32 [2, 128], P('section', 'tensor'), may hold values from -3.6 to 0
- dt_bias: float32 [2, 128], P('section', 'tensor'), may hold values from -4 to -2
- skip_gain: float32 [2, 128], P('section', 'tensor'), may hold values from 0.5 to 2
- out_gain: float32 [2, 8192], P('section', 'tensor'), may hold values from 0.1 to 1.9
Outputs:
- streams_out: bfloat16 [2, 64, 64, 8192], P('section', 'beam', None, 'tensor')
- ssm_out: bfloat16 [2, 64, 128, 64, 128], P('section', 'beam', 'tensor')
- conv_x_out: bfloat16 [2, 64, 3, 8192], P('section', 'beam', None, 'tensor')
- conv_bc_out: bfloat16 [2, 64, 3, 2, 1024], P('section', 'beam', None, None, 'tensor')
The draws below stay inside these ranges and needn't reach their ends.
Inputs may be any that keep to these rules, and one draw needn't show every extreme that they name: `parents`: children 2 k .. 2 k + 1 form block k; each child's parent lies in block k - 1, k or k + 1, blocks counted modulo the number of blocks; in every block the first child takes its parent from the block before and the second child from the block after. `lengths`: some child has all 64 tokens valid in every draw.
All inputs are finite; a program needn't handle non-finite values.
Results may differ from the reference program's by a relative error of at most 0.0055.
Values may be sent and summed in bfloat16 or wider, within the bound.
No kernel may reach another device: no remote copies, remote signals or barrier semaphores. Data moves between devices by JAX's collectives and lax.ppermute only.
A program may use at most 64 MiB of HBM per device.

```python
import math
import jax
import jax.numpy as jnp
from jax import lax

HEADS = 128
HDIM = 64
STATE = 128
CONV = 4
FRESH_SYMBOLS = 64
BEAM_DEV = 2
BEAMS = 64
LAYERS = 2
CH = 8192
GS = 1024


def draw_streams_in(key, part):
    key = jax.random.fold_in(key, 5)
    key_vals, key_rough = jax.random.split(key)
    rough = jax.random.uniform(key_rough, (CH,), minval=0.7, maxval=1.4)
    rising = jnp.exp(jnp.linspace(math.log(0.6), math.log(1.8), CH))
    values = jnp.clip(jax.random.normal(key_vals, (BEAMS, FRESH_SYMBOLS, CH)), -4.0, 4.0)
    return (values * rising * rough).astype(jnp.bfloat16)


def draw_unbiased_increments(key, part):
    key = jax.random.fold_in(key, 7)
    key_noise, key_pos = jax.random.split(key)
    gaussian_perturbation = jnp.clip(0.7 * jax.random.normal(key_noise, (LAYERS, BEAMS, FRESH_SYMBOLS, HEADS)), -3.0, 3.0)
    symbol_locations = jax.random.randint(key_pos, (LAYERS, BEAMS, 3), 0, FRESH_SYMBOLS)
    symbol_group_arrival = jnp.any(jnp.arange(FRESH_SYMBOLS)[None, None, :, None] == symbol_locations[:, :, None, :], axis=3)
    return (gaussian_perturbation + 12.0 * symbol_group_arrival[:, :, :, None].astype(jnp.float32)).astype(jnp.float32)


def draw_a_log(key, part):
    key = jax.random.fold_in(key, 13)
    values = jax.random.uniform(key, (LAYERS, HEADS), minval=math.log(0.03), maxval=0.0)
    return values.astype(jnp.float32)


def draw_parents(key, part):
    key = jax.random.fold_in(key, 11)
    key_step, key_within = jax.random.split(key)
    child = jnp.arange(BEAMS, dtype=jnp.int32)
    blocks = child // BEAM_DEV
    slot = child % BEAM_DEV
    moves = jax.random.randint(key_step, (BEAMS,), -1, 2)
    moves = jnp.where(slot == 0, -1, jnp.where(slot == 1, 1, moves))
    count = BEAMS // BEAM_DEV
    source = (blocks + moves + count) % count
    within = jax.random.randint(key_within, (BEAMS,), 0, BEAM_DEV)
    return (source * BEAM_DEV + within).astype(jnp.int32)


def draw_lengths(key, part):
    key = jax.random.fold_in(key, 23)
    key_counts, key_full = jax.random.split(key)
    counts = jax.random.randint(key_counts, (BEAMS,), 1, FRESH_SYMBOLS + 1)
    full = jax.random.randint(key_full, (), 0, BEAMS)
    return jnp.where(jnp.arange(BEAMS) == full, FRESH_SYMBOLS, counts).astype(jnp.int32)


def block_levels(key, extent, shards, smallest, largest):
    def one(position, shards_of):
        steps = jax.random.uniform(jax.random.fold_in(jax.random.fold_in(key, 6), position), (shards_of,), jnp.float32, smallest / len(shards), largest / len(shards))
        return jnp.repeat(jnp.exp(steps), extent[position] // shards_of).reshape((-1,) + (1,) * (len(extent) - position - 1))

    gain = one(*shards[0])
    for cut in shards[1:]:
        gain = gain * one(*cut)
    return gain


def scatter_about(stream_key, dims, spread, most, shards=(), kind=jnp.bfloat16):
    entries = jax.random.normal(stream_key, dims, jnp.float32) * spread
    if len(shards) > 0:
        entries = block_levels(stream_key, dims, shards, -0.22, 0.18) * entries
    return jnp.clip(entries, min=-most, max=most).astype(kind)


def setup_inputs(seed: int = 0) -> dict:
    keys = jax.random.split(jax.random.key(seed), 16)
    return {
        "streams_in": draw_streams_in(jax.random.fold_in(keys[15], 71), 0),
        "beam_state_cache": scatter_about(keys[1], (LAYERS, BEAMS, HEADS, HDIM, STATE), 1.0, 6.0, ((0, 2), (1, 32), (2, 4))),
        "conv_x_cache": scatter_about(keys[2], (LAYERS, BEAMS, CONV - 1, CH), 1.0, 6.0, ((0, 2), (1, 32), (3, 4))),
        "conv_bc_cache": scatter_about(keys[3], (LAYERS, BEAMS, CONV - 1, 2, GS), 1.0, 6.0, ((0, 2), (1, 32), (4, 4))),
        "bc_inputs": scatter_about(keys[4], (LAYERS, BEAMS, FRESH_SYMBOLS, 2, GS), 1.0, 6.0, ((0, 2), (1, 32), (4, 4))),
        "unbiased_increments": draw_unbiased_increments(jax.random.fold_in(keys[15], 71), 0),
        "parents": draw_parents(jax.random.fold_in(keys[15], 71), 0),
        "lengths": draw_lengths(jax.random.fold_in(keys[15], 71), 0),
        "input_norm_gain": jnp.clip(1.0 + 0.18 * jax.random.normal(keys[8], (LAYERS, CH), jnp.float32), 0.1, 1.9),
        "conv_x_weight": scatter_about(keys[9], (LAYERS, CONV, CH), CONV ** -0.5, 3.0, ((0, 2), (2, 4)), jnp.float32),
        "conv_bc_weight": scatter_about(keys[10], (LAYERS, CONV, 2, GS), CONV ** -0.5, 3.0, ((0, 2), (3, 4)), jnp.float32),
        "a_log": draw_a_log(jax.random.fold_in(keys[15], 71), 0),
        "dt_bias": jnp.clip(-4.0 + 2.0 * jax.random.uniform(keys[12], (LAYERS, HEADS), jnp.float32) ** block_levels(keys[12], (LAYERS, HEADS), ((0, 2), (1, 4)), -0.2, 0.2), -4.0, -2.0),
        "skip_gain": jnp.clip(0.5 + 1.5 * jax.random.uniform(keys[13], (LAYERS, HEADS), jnp.float32) ** block_levels(keys[13], (LAYERS, HEADS), ((0, 2), (1, 4)), -0.2, 0.2), 0.5, 2.0),
        "out_gain": jnp.clip(1.0 + 0.18 * jax.random.normal(keys[14], (LAYERS, CH), jnp.float32), 0.1, 1.9),
    }


EPS = 1e-05
HIGH = lax.Precision.HIGHEST

def convolution_silu(prev, fresh, weight):
    steps = fresh.shape[1]
    whole = jnp.concatenate([prev, fresh], axis=1)
    widened = whole.astype(jnp.float32)
    summed = weight[0] * widened[:, 0:steps]
    for offset in range(1, weight.shape[0]):
        summed = summed + weight[offset] * widened[:, offset:offset + steps]
    return (jax.nn.silu(summed), whole)

def tail_rows(whole, length, keep):
    return jax.vmap(lambda rows, count: lax.dynamic_slice_in_dim(rows, count, keep, 0))(whole, length)

def core(widened, squares, ssm0, conv_x0, conv_bc0, bc_new, dt_raw, length, gain_in, weight_x, weight_bc, log_rate, bias_dt, skip, gain_out):
    beams, steps, chans = widened.shape
    heads = dt_raw.shape[2]
    hdim = chans // heads
    scale = lax.rsqrt(squares / CH + EPS)
    x_in = (widened * scale[:, :, None] * gain_in).astype(jnp.bfloat16)
    x_conv, whole_x = convolution_silu(conv_x0, x_in, weight_x)
    bc_conv, whole_bc = convolution_silu(conv_bc0, bc_new, weight_bc)
    places = jnp.arange(steps, dtype=jnp.int32)
    valid = (places[None, :] < length[:, None]).astype(jnp.float32)
    x_vals = x_conv * valid[:, :, None]
    groups = bc_conv.shape[3] // STATE
    per_group = heads // groups
    b_mat = bc_conv[:, :, 0].reshape(beams, steps, groups, STATE)
    c_mat = bc_conv[:, :, 1].reshape(beams, steps, groups, STATE)
    step_dt = jax.nn.softplus(dt_raw + bias_dt) * valid[:, :, None]
    cum = jnp.cumsum(-step_dt * jnp.exp(log_rate), axis=1)
    x_heads = x_vals.reshape(beams, steps, heads, hdim)
    inner = jnp.einsum('btgn,bsgn->bgts', c_mat, b_mat, precision=HIGH)
    inner = jnp.repeat(inner, per_group, axis=1)
    cum_t = jnp.transpose(cum, (0, 2, 1))
    causal = places[:, None] >= places[None, :]
    gap = cum_t[:, :, :, None] - cum_t[:, :, None, :]
    decay = jnp.where(causal, jnp.exp(jnp.where(causal, gap, 0.0)), 0.0)
    mixing = decay * inner * jnp.transpose(step_dt, (0, 2, 1))[:, :, None, :]
    y_out = jnp.einsum('bhts,bshp->bthp', mixing, x_heads, precision=HIGH)
    readout_per_head = jnp.repeat(c_mat, per_group, axis=2)
    start = ssm0.astype(jnp.float32)
    y_out = y_out + jnp.exp(cum)[:, :, :, None] * jnp.einsum('bthn,bhpn->bthp', readout_per_head, start, precision=HIGH)
    y_out = y_out + skip[None, None, :, None] * x_heads
    grouped = y_out.reshape(beams, steps, groups, per_group * hdim)
    normed = grouped * lax.rsqrt(lax.optimization_barrier(jnp.mean(grouped * grouped, axis=3, keepdims=True)) + EPS)
    normed = normed.reshape(beams, steps, chans) * gain_out
    h_out = (widened + normed * valid[:, :, None]).astype(jnp.bfloat16)
    final = cum[:, -1]
    weights = jnp.exp(final[:, None, :] - cum) * step_dt
    b_heads = jnp.repeat(b_mat, per_group, axis=2)
    s_new = jnp.exp(final)[:, :, None, None] * start + jnp.einsum('bthp,bthn->bhpn', x_heads * weights[:, :, :, None], b_heads, precision=HIGH)
    keep = conv_x0.shape[1]
    return (h_out, s_new.astype(jnp.bfloat16), tail_rows(whole_x, length, keep), tail_rows(whole_bc, length, keep))

def reference(streams_in, beam_state_cache, conv_x_cache, conv_bc_cache, bc_inputs, unbiased_increments, parents, lengths, input_norm_gain, conv_x_weight, conv_bc_weight, a_log, dt_bias, skip_gain, out_gain):
    collected = ([], [], [], [])
    hidden = streams_in
    for layer in range(LAYERS):
        ssm_par = beam_state_cache[layer][parents]
        conv_x_par = conv_x_cache[layer][parents]
        conv_bc_par = conv_bc_cache[layer][parents]

        def one_beam(items):
            h_row, s_row, cx_row, convolved_bc_row, bc_row, increment_vector, count = items
            widened = h_row[None].astype(jnp.float32)
            squares = lax.optimization_barrier(jnp.sum(widened * widened, axis=2))
            result = core(widened, squares, s_row[None], cx_row[None], convolved_bc_row[None], bc_row[None], increment_vector[None], count[None], input_norm_gain[layer], conv_x_weight[layer], conv_bc_weight[layer], a_log[layer], dt_bias[layer], skip_gain[layer], out_gain[layer])
            return tuple((part[0] for part in result))
        result = lax.map(one_beam, (hidden, ssm_par, conv_x_par, conv_bc_par, bc_inputs[layer], unbiased_increments[layer], lengths))
        for store, part in zip(collected, result):
            store.append(part)
        hidden = result[0]
    return (jnp.stack(collected[0]), jnp.stack(collected[1]), jnp.stack(collected[2]), jnp.stack(collected[3]))
```

```python
import functools

import jax
import jax.numpy as jnp
from jax import lax
from jax.experimental import pallas as pl
from jax.experimental.pallas import tpu as pltpu
from jax.sharding import PartitionSpec as P

CH = 8192
EPS = 1e-05
KIDS = 2
T = 64
CD = 2048
HD = 32
N = 128
GC = 1024
F32 = jnp.float32
BF16 = jnp.bfloat16
HIGHEST = lax.Precision.HIGHEST
VMEM = pl.BlockSpec(memory_space=pltpu.VMEM)
SMEM = pl.BlockSpec(memory_space=pltpu.SMEM)
ANY = pl.BlockSpec(memory_space=pl.ANY)


def iota(shape, dim):
    return lax.broadcasted_iota(jnp.int32, shape, dim)


def as_row(col):
    size = col.shape[0]
    keep = iota((size, size), 0) == iota((size, size), 1)
    return jnp.sum(jnp.where(keep, col, 0.0), axis=0, keepdims=True)


def as_col(row):
    size = row.shape[1]
    keep = iota((size, size), 0) == iota((size, size), 1)
    return jnp.sum(jnp.where(keep, row, 0.0), axis=1, keepdims=True)


def silu(v):
    return 0.5 * v * (1.0 + jnp.tanh(0.5 * v))


def dot(a, b, dims, precision=None):
    return lax.dot_general(
        a, b, (dims, ((), ())), precision=precision, preferred_element_type=F32
    )


def three_parts(v):
    high = v.astype(BF16)
    rest = v - high.astype(F32)
    mid = rest.astype(BF16)
    low = (rest - mid.astype(F32)).astype(BF16)
    return [high, mid, low]


def pick_kernel(pick_ref, stream_ref, state_ref, part_ref, fwd_ref, bwd_ref, sems):
    first = pltpu.make_async_copy(state_ref.at[pick_ref[0]], fwd_ref, sems.at[0])
    second = pltpu.make_async_copy(state_ref.at[pick_ref[1]], bwd_ref, sems.at[1])
    first.start()
    second.start()
    for c in range(KIDS):
        s = stream_ref[c].astype(F32)
        part_ref[c : c + 1, :] = as_row(jnp.sum(s * s, axis=1, keepdims=True))
    first.wait()
    second.wait()


def fresh_x(s, total, rows, gain, taps, valid, px_ref):
    scale = lax.rsqrt(total / CH + EPS)
    x_in = (s * scale * gain).astype(BF16).astype(F32)
    px_ref[5:8, :] = rows.astype(F32)
    px_ref[8:72, :] = x_in
    acc = taps[0:1] * px_ref[5:69, :]
    for k in range(1, 4):
        acc = acc + taps[k : k + 1] * px_ref[5 + k : 69 + k, :]
    return silu(acc) * valid


def intra(mix_ref, c, x):
    xb = x.astype(BF16)
    outs = []
    lane = iota((T, 256), 1) // 64
    masks = [jnp.where(lane == j, 1.0, 0.0).astype(BF16) for j in range(4)]
    for q in range(CD // 256):
        xq = xb[:, 256 * q : 256 * (q + 1)]
        rhs = jnp.concatenate([xq * mask for mask in masks], axis=0)
        outs.append(dot(mix_ref[c, :, 256 * q : 256 * (q + 1)], rhs, ((1,), (0,))))
    return jnp.concatenate(outs, axis=1)


def finish(y, s, gain, valid):
    outs = []
    for g in range(CD // GC):
        part = y[:, GC * g : GC * (g + 1)]
        mean = jnp.sum(part * part, axis=1, keepdims=True) * (1.0 / GC)
        outs.append(part * lax.rsqrt(mean + EPS))
    z = jnp.concatenate(outs, axis=1) * gain
    return (s + z * valid).astype(BF16)


def valid_col(length):
    return jnp.where(iota((T, 1), 0) < length, 1.0, 0.0)


def pre_kernel(
    len_ref,
    rows_b_ref,
    rows_a_ref,
    bc_ref,
    inc_ref,
    taps_bc_ref,
    log_ref,
    bias_ref,
    stream_ref,
    p0_ref,
    p1_ref,
    p2_ref,
    p3_ref,
    gain_ref,
    taps_ref,
    skip_ref,
    mix_ref,
    weight_ref,
    grow_ref,
    b_ref,
    c_ref,
    last_ref,
    y_ref,
    bc_out_ref,
    pbc_ref,
    px_ref,
):
    rate = as_col(jnp.exp(log_ref[...]))
    bias = as_col(bias_ref[...])
    upper = jnp.where(iota((T, T), 0) <= iota((T, T), 1), 1.0, 0.0)
    onehot = jnp.where(iota((HD, CD), 0) == iota((HD, CD), 1) // 64, 1.0, 0.0).astype(BF16)
    onehot = jnp.concatenate([onehot] * 3, axis=0)
    diag = iota((T, CD), 1) % T == iota((T, CD), 0)
    causal = iota((T, N), 0) >= iota((T, N), 1) % T
    totals = p0_ref[...] + p1_ref[...] + p2_ref[...] + p3_ref[...]
    for c in range(KIDS):
        length = len_ref[c]
        rows_ref = (rows_b_ref, rows_a_ref)[c]
        rows = rows_ref[...]
        pbc_ref[5:8, :] = rows[:, CD:].astype(F32)
        pbc_ref[8:72, :] = bc_ref[c].astype(F32)
        taps = [
            jnp.concatenate([taps_bc_ref[k, 0:1, :], taps_bc_ref[k, 1:2, :]], axis=1)
            for k in range(4)
        ]
        acc = taps[0] * pbc_ref[5:69, :]
        for k in range(1, 4):
            acc = acc + taps[k] * pbc_ref[5 + k : 69 + k, :]
        bc = silu(acc)
        for k in range(3):
            row = pbc_ref[pl.ds(5 + length + k, 1), :]
            bc_out_ref[c, k] = jnp.concatenate([row[:, :256], row[:, 256:]], axis=0).astype(BF16)
        b_ref[c] = bc[:, :256].astype(BF16)
        c_ref[c] = bc[:, 256:].astype(BF16)
        valid_row = jnp.where(iota((1, T), 1) < length, 1.0, 0.0)
        raw = inc_ref[c] + bias
        dt = (jnp.maximum(raw, 0.0) + jnp.log1p(jnp.exp(-jnp.abs(raw)))) * valid_row
        cum = dot(-dt * rate, upper, ((1,), (0,)), HIGHEST)
        last_ref[c] = jnp.broadcast_to(jnp.exp(cum[:, T - 1 : T]), (HD, N))
        edt = dot(jnp.concatenate(three_parts(dt), axis=0), onehot, ((0,), (0,)))
        ecum = dot(jnp.concatenate(three_parts(cum), axis=0), onehot, ((0,), (0,)))
        row_dt = jnp.sum(jnp.where(diag, edt, 0.0), axis=0, keepdims=True)
        row_cum = jnp.sum(jnp.where(diag, ecum, 0.0), axis=0, keepdims=True)
        grow_ref[c] = jnp.exp(ecum)
        weight_ref[c] = jnp.exp(ecum[T - 1 : T] - ecum) * edt
        for g in range(2):
            bg = bc[:, N * g : N * (g + 1)]
            cg = bc[:, 256 + N * g : 256 + N * (g + 1)]
            inner = dot(cg, jnp.concatenate([bg, bg], axis=0), ((1,), (1,)), HIGHEST)
            inner = jnp.where(causal, inner, 0.0)
            for j in range(8 * g, 8 * g + 8):
                at = slice(N * j, N * (j + 1))
                gap = jnp.minimum(ecum[:, at] - row_cum[:, at], 0.0)
                mix_ref[c, :, at] = (jnp.exp(gap) * inner * row_dt[:, at]).astype(BF16)
        s = stream_ref[c].astype(F32)
        x = fresh_x(
            s,
            as_col(totals[c : c + 1]),
            rows[:, :CD],
            gain_ref[...],
            taps_ref[...],
            valid_col(length),
            px_ref,
        )
        y_ref[c] = intra(mix_ref, c, x) + skip_ref[...] * x


def mid_kernel(
    len_ref,
    y_ref,
    grow_ref,
    c_ref,
    state_b_ref,
    state_a_ref,
    stream_ref,
    gain_ref,
    out_ref,
    part_ref,
    read_ref,
):
    for c in range(KIDS):
        state_ref = (state_b_ref, state_a_ref)[c]
        read = jnp.concatenate(
            [
                dot(c_ref[c, :, N * g : N * (g + 1)], state_ref[GC * g : GC * (g + 1), :], ((1,), (1,)))
                for g in range(2)
            ],
            axis=1,
        )
        read = read * grow_ref[c]
        read_ref[c] = read
        out = finish(
            y_ref[c] + read, stream_ref[c].astype(F32), gain_ref[...], valid_col(len_ref[c])
        )
        out_ref[c] = out
        s = out.astype(F32)
        part_ref[c : c + 1, :] = as_row(jnp.sum(s * s, axis=1, keepdims=True))


def last_kernel(
    len_ref,
    sec_ref,
    stream_ref,
    moved_ref,
    r1_ref,
    r2_ref,
    r3_ref,
    q1_ref,
    q2_ref,
    q3_ref,
    rows_b_ref,
    rows_a_ref,
    gain_in_ref,
    taps_ref,
    skip_ref,
    gain_ref,
    mix_ref,
    weight_ref,
    read_ref,
    b_ref,
    last_ref,
    state_b_ref,
    state_a_ref,
    out_ref,
    new_ref,
    x_out_ref,
    px_ref,
):
    first = sec_ref[0] == 0
    others = jnp.where(
        first,
        r1_ref[...] + r2_ref[...] + r3_ref[...],
        q1_ref[...] + q2_ref[...] + q3_ref[...],
    )
    tails = []
    for c in range(KIDS):
        length = len_ref[c]
        valid = valid_col(length)
        rows_ref = (rows_b_ref, rows_a_ref)[c]
        state_ref = (state_b_ref, state_a_ref)[c]
        s = jnp.where(first, stream_ref[c].astype(F32), moved_ref[c].astype(F32))
        total = jnp.sum(s * s, axis=1, keepdims=True) + as_col(others[c : c + 1])
        x = fresh_x(s, total, rows_ref[:, :CD], gain_in_ref[...], taps_ref[...], valid, px_ref)
        tails.append([px_ref[pl.ds(5 + length + k, 1), :] for k in range(3)])
        y = intra(mix_ref, c, x) + skip_ref[...] * x + read_ref[c]
        out_ref[c] = finish(y, s, gain_ref[...], valid)
        xw = (x * weight_ref[c]).astype(BF16)
        for g in range(2):
            fresh = dot(xw[:, GC * g : GC * (g + 1)], b_ref[c, :, N * g : N * (g + 1)], ((0,), (0,)))
            for h in range(16 * g, 16 * g + 16):
                at = slice(64 * h, 64 * (h + 1))
                off = 64 * (h - 16 * g)
                new_ref[c, at, :] = (
                    last_ref[c, h : h + 1, :] * state_ref[at, :].astype(F32) + fresh[off : off + 64]
                ).astype(BF16)
    for k in range(3):
        x_out_ref[k] = jnp.concatenate([tails[0][k], tails[1][k]], axis=0).astype(BF16)


def shape(dims, kind):
    return jax.ShapeDtypeStruct(dims, kind)


def params(mib):
    return pltpu.CompilerParams(vmem_limit_bytes=mib * 2**20)


def cost(flops, moved, exps=0):
    return pl.CostEstimate(flops=flops, bytes_accessed=moved, transcendentals=exps)


def on_device(
    streams_in,
    beam_state_cache,
    conv_x_cache,
    conv_bc_cache,
    bc_inputs,
    unbiased_increments,
    parents,
    lengths,
    input_norm_gain,
    conv_x_weight,
    conv_bc_weight,
    a_log,
    dt_bias,
    skip_gain,
    out_gain,
):
    peers = lax.axis_size("beam")
    me = lax.axis_index("beam")
    tens = lax.axis_size("tensor")
    section = lax.axis_index("section").astype(jnp.int32)
    pick = jnp.stack(
        [
            parents[KIDS * ((me + 1) % peers)] % KIDS,
            parents[KIDS * ((me + peers - 1) % peers) + 1] % KIDS,
        ]
    ).astype(jnp.int32)
    states = beam_state_cache[0].reshape(KIDS, CD, N)
    part, fwd, bwd = pl.pallas_call(
        pick_kernel,
        out_shape=(shape((KIDS, T), F32), shape((CD, N), BF16), shape((CD, N), BF16)),
        in_specs=[SMEM, VMEM, ANY],
        out_specs=(VMEM, ANY, ANY),
        scratch_shapes=[pltpu.SemaphoreType.DMA((2,))],
        compiler_params=params(8),
        name="pick",
    )(pick, streams_in, states)

    def along(value, axis, steps):
        size = lax.axis_size(axis)
        return lax.ppermute(value, axis, [(i, (i + steps) % size) for i in range(size)])

    packed = jnp.concatenate(
        [conv_x_cache[0], conv_bc_cache[0].reshape(KIDS, 3, 512)], axis=2
    )
    rows_b = along(lax.dynamic_index_in_dim(packed, pick[0], 0, False), "beam", 1)
    rows_a = along(lax.dynamic_index_in_dim(packed, pick[1], 0, False), "beam", -1)
    r1, r2, r3 = [along(part, "tensor", k) for k in range(1, tens)]
    state_b = along(fwd, "beam", 1)
    state_a = along(bwd, "beam", -1)

    bc = bc_inputs[0].reshape(KIDS, T, 512)
    inc = jnp.transpose(unbiased_increments[0], (0, 2, 1))
    skip = jnp.repeat(skip_gain, 64, axis=1)
    taps = conv_x_weight[0]
    mix, weight, grow, b_mat, c_mat, last, y_part, bc_out = pl.pallas_call(
        pre_kernel,
        out_shape=(
            shape((KIDS, T, CD), BF16),
            shape((KIDS, T, CD), F32),
            shape((KIDS, T, CD), F32),
            shape((KIDS, T, 256), BF16),
            shape((KIDS, T, 256), BF16),
            shape((KIDS, HD, N), F32),
            shape((KIDS, T, CD), F32),
            shape((KIDS, 3, 2, 256), BF16),
        ),
        in_specs=[SMEM] + [VMEM] * 15,
        out_specs=tuple([VMEM] * 8),
        scratch_shapes=[pltpu.VMEM((72, 512), F32), pltpu.VMEM((72, CD), F32)],
        compiler_params=params(24),
        cost_estimate=cost(200_000_000, 5_000_000, 1_000_000),
        name="pre",
    )(
        lengths,
        rows_b,
        rows_a,
        bc,
        inc,
        conv_bc_weight[0],
        a_log,
        dt_bias,
        streams_in,
        part,
        r1,
        r2,
        r3,
        input_norm_gain,
        taps,
        skip,
    )
    mid, mid_part, read = pl.pallas_call(
        mid_kernel,
        out_shape=(
            shape((KIDS, T, CD), BF16),
            shape((KIDS, T), F32),
            shape((KIDS, T, CD), F32),
        ),
        in_specs=[SMEM] + [VMEM] * 7,
        out_specs=(VMEM, VMEM, VMEM),
        compiler_params=params(16),
        name="mid",
    )(lengths, y_part, grow, c_mat, state_b, state_a, streams_in, out_gain)

    moved = lax.ppermute(mid, "section", [(0, 1)])
    q1, q2, q3 = [
        lax.ppermute(
            mid_part, ("section", "tensor"), [(i, tens + (i + k) % tens) for i in range(tens)]
        )
        for k in range(1, tens)
    ]
    out, new, x_out = pl.pallas_call(
        last_kernel,
        out_shape=(
            shape((KIDS, T, CD), BF16),
            shape((KIDS, CD, N), BF16),
            shape((3, KIDS, CD), BF16),
        ),
        in_specs=[SMEM, SMEM] + [VMEM] * 21,
        out_specs=(VMEM, VMEM, VMEM),
        scratch_shapes=[pltpu.VMEM((72, CD), F32)],
        compiler_params=params(24),
        name="last",
    )(
        lengths,
        section[None],
        streams_in,
        moved,
        r1,
        r2,
        r3,
        q1,
        q2,
        q3,
        rows_b,
        rows_a,
        input_norm_gain,
        taps,
        skip,
        out_gain,
        mix,
        weight,
        read,
        b_mat,
        last,
        state_b,
        state_a,
    )
    return (
        out[None],
        new.reshape(1, KIDS, HD, 64, N),
        jnp.transpose(x_out, (1, 0, 2))[None],
        bc_out[None],
    )


def solution(mesh):
    placed = (
        P("beam", None, "tensor"),
        P("section", "beam", "tensor", None, None),
        P("section", "beam", None, "tensor"),
        P("section", "beam", None, None, "tensor"),
        P("section", "beam", None, None, "tensor"),
        P("section", "beam", None, "tensor"),
        P(),
        P("beam"),
        P("section", "tensor"),
        P("section", None, "tensor"),
        P("section", None, None, "tensor"),
        P("section", "tensor"),
        P("section", "tensor"),
        P("section", "tensor"),
        P("section", "tensor"),
    )
    return jax.shard_map(
        on_device,
        mesh=mesh,
        in_specs=placed,
        out_specs=(
            P("section", "beam", None, "tensor"),
            P("section", "beam", "tensor", None, None),
            P("section", "beam", None, "tensor"),
            P("section", "beam", None, None, "tensor"),
        ),
        check_vma=False,
    )
```

```python
import functools

import jax
import jax.numpy as jnp
from jax import lax
from jax.experimental import pallas as pl
from jax.experimental.pallas import tpu as pltpu
from jax.sharding import PartitionSpec as P

CH = 8192
EPS = 1e-05
KIDS = 2
T = 64
CD = 2048
HD = 32
N = 128
GC = 1024
F32 = jnp.float32
BF16 = jnp.bfloat16
HIGHEST = lax.Precision.HIGHEST
VMEM = pl.BlockSpec(memory_space=pltpu.VMEM)
SMEM = pl.BlockSpec(memory_space=pltpu.SMEM)
HBM = pl.BlockSpec(memory_space=pl.ANY)
BIG = 60


def iota(shape, dim):
    return lax.broadcasted_iota(jnp.int32, shape, dim)


def as_row(col):
    size = col.shape[0]
    keep = iota((size, size), 0) == iota((size, size), 1)
    return jnp.sum(jnp.where(keep, col, 0.0), axis=0, keepdims=True)


def as_col(row):
    size = row.shape[1]
    keep = iota((size, size), 0) == iota((size, size), 1)
    return jnp.sum(jnp.where(keep, row, 0.0), axis=1, keepdims=True)


def silu(v):
    return 0.5 * v * (1.0 + jnp.tanh(0.5 * v))


def dot(a, b, dims, precision=None):
    return lax.dot_general(
        a, b, (dims, ((), ())), precision=precision, preferred_element_type=F32
    )


def three_parts(v):
    high = v.astype(BF16)
    rest = v - high.astype(F32)
    mid = rest.astype(BF16)
    low = (rest - mid.astype(F32)).astype(BF16)
    return [high, mid, low]


def pick_kernel(
    parents_in_ref,
    conv_x_in_ref,
    conv_bc_in_ref,
    state_in_ref,
    one_ref,
    two_ref,
    parents_ref,
    conv_x_ref,
    conv_bc_ref,
    state_ref,
    rows_ref,
    sems,
    out_sems,
):
    get_parents = pltpu.make_async_copy(parents_in_ref, parents_ref, sems.at[0])
    get_states = [
        pltpu.make_async_copy(state_in_ref.at[i], state_ref.at[i], sems.at[1 + i])
        for i in range(KIDS)
    ]
    get_x = pltpu.make_async_copy(conv_x_in_ref, conv_x_ref, sems.at[3])
    get_bc = pltpu.make_async_copy(conv_bc_in_ref, conv_bc_ref, sems.at[4])
    for copy in (get_parents, *get_states, get_x, get_bc):
        copy.start()
    peers = lax.axis_size("beam")
    me = lax.axis_index("beam")
    get_parents.wait()
    picks = (
        lax.rem(parents_ref[KIDS * lax.rem(me + 1, peers)], KIDS),
        lax.rem(parents_ref[KIDS * lax.rem(me + peers - 1, peers) + 1], KIDS),
    )
    outs = (one_ref, two_ref)
    for copy in get_states:
        copy.wait()
    puts = []
    for i in range(2):
        puts.append(
            pltpu.make_async_copy(state_ref.at[picks[i]], outs[i].at[:CD], out_sems.at[0, i])
        )
        puts[-1].start()
    get_x.wait()
    get_bc.wait()
    for i in range(2):
        low = picks[i] == 0
        pieces = []
        for k in range(3):
            both = conv_x_ref[k].astype(F32)
            row = jnp.where(low, both[0:1], both[1:2])
            pieces += [row[:, N * j : N * (j + 1)] for j in range(CD // N)]
        for k in range(3):
            both = conv_bc_ref[picks[i], k].astype(F32)
            pieces += [both[p : p + 1, N * j : N * (j + 1)] for p in range(2) for j in range(2)]
        pieces.append(jnp.zeros((4, N), F32))
        rows_ref[i] = jnp.concatenate(pieces, axis=0).astype(BF16)
        puts.append(pltpu.make_async_copy(rows_ref.at[i], outs[i].at[CD:], out_sems.at[1, i]))
        puts[-1].start()
    for copy in puts:
        copy.wait()


def square_kernel(stream_ref, part_ref):
    for c in range(KIDS):
        s = stream_ref[c].astype(F32)
        part_ref[c : c + 1, :] = as_row(jnp.sum(s * s, axis=1, keepdims=True))


def fresh_x(s, total, rows, gain, taps, valid, px_ref):
    scale = lax.rsqrt(total / CH + EPS)
    for k in range(3):
        for j in range(CD // N):
            at = 16 * k + j
            px_ref[5 + k : 6 + k, N * j : N * (j + 1)] = rows[at : at + 1, :]
    px_ref[8:72, :] = (s * scale * gain).astype(BF16).astype(F32)
    acc = taps[0:1] * px_ref[5:69, :]
    for k in range(1, 4):
        acc = acc + taps[k : k + 1] * px_ref[5 + k : 69 + k, :]
    return silu(acc) * valid


def fresh_bc(rows, bc, taps_ref, pbc_ref):
    for k in range(3):
        for j in range(4):
            at = 48 + 4 * k + j
            pbc_ref[5 + k : 6 + k, N * j : N * (j + 1)] = rows[at : at + 1, :]
    pbc_ref[8:72, :] = bc.astype(F32)
    acc = 0.0
    for k in range(4):
        taps = jnp.concatenate([taps_ref[k, 0:1, :], taps_ref[k, 1:2, :]], axis=1)
        acc = acc + taps * pbc_ref[5 + k : 69 + k, :]
    return silu(acc)


def mixing(bc, decay_ref, mix_ref):
    for g in range(2):
        bg = bc[:, N * g : N * (g + 1)]
        cg = bc[:, 256 + N * g : 256 + N * (g + 1)]
        inner = dot(cg, jnp.concatenate([bg, bg], axis=0), ((1,), (1,)), HIGHEST)
        for j in range(8 * g, 8 * g + 8):
            at = slice(N * j, N * (j + 1))
            mix_ref[:, at] = (decay_ref[:, at] * inner).astype(BF16)


def readout(bc, state, grow):
    cb = bc[:, 256:].astype(BF16)
    read = [
        dot(cb[:, N * g : N * (g + 1)], state[GC * g : GC * (g + 1), :], ((1,), (1,)))
        for g in range(2)
    ]
    return jnp.concatenate(read, axis=1) * grow


def intra(mix_ref, x):
    xb = x.astype(BF16)
    outs = []
    lane = iota((T, 256), 1) // 64
    masks = [jnp.where(lane == j, 1.0, 0.0).astype(BF16) for j in range(4)]
    for q in range(CD // 256):
        xq = xb[:, 256 * q : 256 * (q + 1)]
        rhs = jnp.concatenate([xq * mask for mask in masks], axis=0)
        outs.append(dot(mix_ref[:, 256 * q : 256 * (q + 1)], rhs, ((1,), (0,))))
    return jnp.concatenate(outs, axis=1)


def finish(y, s, gain, valid):
    outs = []
    for g in range(CD // GC):
        part = y[:, GC * g : GC * (g + 1)]
        mean = jnp.sum(part * part, axis=1, keepdims=True) * (1.0 / GC)
        outs.append(part * lax.rsqrt(mean + EPS))
    z = jnp.concatenate(outs, axis=1) * gain
    return (s + z * valid).astype(BF16)


def valid_col(length):
    return jnp.where(iota((T, 1), 0) < length, 1.0, 0.0)


def spread_heads(compact):
    onehot = jnp.where(iota((HD, CD), 0) == iota((HD, CD), 1) // 64, 1.0, 0.0).astype(BF16)
    onehot = jnp.concatenate([onehot] * 3, axis=0)
    return dot(jnp.concatenate(three_parts(compact), axis=0), onehot, ((0,), (0,)))


def pre_kernel(
    len_ref, inc_ref, log_ref, bias_ref, decay0_ref, decay1_ref, grow_ref, weight_ref, last_ref
):
    rate = as_col(jnp.exp(log_ref[...]))
    bias = as_col(bias_ref[...])
    upper = jnp.where(iota((T, T), 0) <= iota((T, T), 1), 1.0, 0.0)
    diag = iota((T, CD), 1) % T == iota((T, CD), 0)
    causal = iota((T, CD), 0) >= iota((T, CD), 1) % T
    for c in range(KIDS):
        valid_row = jnp.where(iota((1, T), 1) < len_ref[c], 1.0, 0.0)
        raw = inc_ref[c] + bias
        dt = (jnp.maximum(raw, 0.0) + jnp.log1p(jnp.exp(-jnp.abs(raw)))) * valid_row
        cum = dot(-dt * rate, upper, ((1,), (0,)), HIGHEST)
        final = cum[:, T - 1 : T]
        last_ref[c] = jnp.broadcast_to(jnp.exp(final), (HD, N))
        grow_ref[c] = jnp.exp(cum)
        weight_ref[c] = jnp.exp(final - cum) * dt
        edt = spread_heads(dt)
        ecum = spread_heads(cum)
        row_dt = jnp.sum(jnp.where(diag, edt, 0.0), axis=0, keepdims=True)
        row_cum = jnp.sum(jnp.where(diag, ecum, 0.0), axis=0, keepdims=True)
        gap = jnp.exp(jnp.minimum(ecum - row_cum, 0.0))
        (decay0_ref, decay1_ref)[c][...] = jnp.where(causal, gap * row_dt, 0.0)


def mid_kernel(
    c,
    len_ref,
    message_ref,
    bc_ref,
    taps_bc_ref,
    stream_ref,
    p0_ref,
    p1_ref,
    p2_ref,
    p3_ref,
    gain_in_ref,
    taps_ref,
    skip_ref,
    gain_ref,
    decay_ref,
    grow_ref,
    *refs,
):
    if c == 1:
        early_ref, early_part_ref, early_bc_ref = refs[:3]
        refs = refs[3:]
    out_ref, part_ref, bc_out_ref, mix_ref, read_ref, b_ref = refs[:6]
    pbc_ref, px_ref = refs[6:]
    length = len_ref[c]
    rows = message_ref[CD:, :].astype(F32)
    bc = fresh_bc(rows, bc_ref[c], taps_bc_ref, pbc_ref)
    if c == 1:
        bc_out_ref[0] = early_bc_ref[0]
    for k in range(3):
        row = pbc_ref[pl.ds(5 + length + k, 1), :]
        bc_out_ref[c, k] = jnp.concatenate([row[:, :256], row[:, 256:]], axis=0).astype(BF16)
    b_ref[...] = bc[:, :256].astype(BF16)
    read = readout(bc, message_ref[:CD, :], spread_heads(grow_ref[c]))
    read_ref[...] = read.astype(BF16)
    mixing(bc, decay_ref, mix_ref)
    s = stream_ref[c].astype(F32)
    valid = valid_col(length)
    total = p0_ref[c : c + 1] + p1_ref[c : c + 1] + p2_ref[c : c + 1] + p3_ref[c : c + 1]
    x = fresh_x(s, as_col(total), rows, gain_in_ref[...], taps_ref[...], valid, px_ref)
    y = intra(mix_ref, x) + skip_ref[...] * x + read
    out = finish(y, s, gain_ref[...], valid)
    s = out.astype(F32)
    part = as_row(jnp.sum(s * s, axis=1, keepdims=True))
    if c == 0:
        out_ref[...] = out
        part_ref[...] = part
    else:
        out_ref[0] = early_ref[...]
        out_ref[1] = out
        part_ref[0:1, :] = early_part_ref[...]
        part_ref[1:2, :] = part


def others_kernel(sec_ref, r1_ref, r2_ref, r3_ref, q1_ref, q2_ref, q3_ref, others_ref):
    others_ref[...] = jnp.where(
        sec_ref[0] == 0,
        r1_ref[...] + r2_ref[...] + r3_ref[...],
        q1_ref[...] + q2_ref[...] + q3_ref[...],
    )


def last_kernel(
    sec_ref,
    len_ref,
    others_ref,
    gain_in_ref,
    taps_ref,
    skip_ref,
    gain_ref,
    b0_ref,
    b1_ref,
    last_ref,
    stream_ref,
    moved_ref,
    weight_ref,
    mix0_ref,
    mix1_ref,
    read0_ref,
    read1_ref,
    message0_in_ref,
    message1_in_ref,
    out_in_ref,
    new_in_ref,
    x_out_ref,
    px_ref,
    message_ref,
    out_ref,
    new_ref,
    sems,
):
    first = sec_ref[0] == 0

    gets = []
    puts = []
    for c in range(KIDS):
        gets.append(
            pltpu.make_async_copy(
                (message0_in_ref, message1_in_ref)[c], message_ref.at[c], sems.at[0, c]
            )
        )
        gets[c].start()
        puts.append(pltpu.make_async_copy(out_ref.at[c], out_in_ref.at[c], sems.at[1, c]))
        puts.append(pltpu.make_async_copy(new_ref.at[c], new_in_ref.at[c], sems.at[2, c]))
    tails = []
    for c in range(KIDS):
        length = len_ref[c]
        valid = valid_col(length)
        b_ref = (b0_ref, b1_ref)[c]
        s = jnp.where(first, stream_ref[c].astype(F32), moved_ref[c].astype(F32))
        total = jnp.sum(s * s, axis=1, keepdims=True) + as_col(others_ref[c : c + 1])
        gets[c].wait()
        rows = message_ref[c, CD:, :].astype(F32)
        x = fresh_x(s, total, rows, gain_in_ref[...], taps_ref[...], valid, px_ref)
        tails.append([px_ref[pl.ds(5 + length + k, 1), :] for k in range(3)])
        y = intra((mix0_ref, mix1_ref)[c], x) + skip_ref[...] * x
        y = y + (read0_ref, read1_ref)[c][...].astype(F32)
        out_ref[c] = finish(y, s, gain_ref[...], valid)
        puts[2 * c].start()
        xw = (x * spread_heads(weight_ref[c])).astype(BF16)
        for g in range(2):
            fresh = dot(xw[:, GC * g : GC * (g + 1)], b_ref[:, N * g : N * (g + 1)], ((0,), (0,)))
            for h in range(16 * g, 16 * g + 16):
                at = slice(64 * h, 64 * (h + 1))
                off = 64 * (h - 16 * g)
                new_ref[c, at, :] = (
                    last_ref[c, h : h + 1, :] * message_ref[c, at, :].astype(F32)
                    + fresh[off : off + 64]
                ).astype(BF16)
        puts[2 * c + 1].start()
    for k in range(3):
        x_out_ref[k] = jnp.concatenate([tails[0][k], tails[1][k]], axis=0).astype(BF16)
    for copy in puts:
        copy.wait()


def shape(dims, kind):
    return jax.ShapeDtypeStruct(dims, kind)


def params(mib):
    return pltpu.CompilerParams(vmem_limit_bytes=mib * 2**20)


def cost(flops, moved, exps=0):
    return pl.CostEstimate(flops=flops, bytes_accessed=moved, transcendentals=exps)


def on_device(
    streams_in,
    beam_state_cache,
    conv_x_cache,
    conv_bc_cache,
    bc_inputs,
    unbiased_increments,
    parents,
    lengths,
    input_norm_gain,
    conv_x_weight,
    conv_bc_weight,
    a_log,
    dt_bias,
    skip_gain,
    out_gain,
):
    tens = lax.axis_size("tensor")
    peers = lax.axis_size("beam")
    section = lax.axis_index("section").astype(jnp.int32)[None]
    message = shape((CD + 64, N), BF16)
    fwd, bwd = pl.pallas_call(
        pick_kernel,
        out_shape=(message, message),
        in_specs=[HBM] * 4,
        out_specs=(HBM, HBM),
        scratch_shapes=[
            pltpu.SMEM(parents.shape, jnp.int32),
            pltpu.VMEM((3, KIDS, CD), BF16),
            pltpu.VMEM((KIDS, 3, 2, 256), BF16),
            pltpu.VMEM((KIDS, CD, N), BF16),
            pltpu.VMEM((2, 64, N), BF16),
            pltpu.SemaphoreType.DMA((5,)),
            pltpu.SemaphoreType.DMA((2, 2)),
        ],
        compiler_params=params(BIG),
        name="pick",
    )(
        parents,
        jnp.transpose(conv_x_cache[0], (1, 0, 2)),
        conv_bc_cache[0],
        beam_state_cache[0].reshape(KIDS, CD, N),
    )
    part = pl.pallas_call(
        square_kernel,
        out_shape=shape((KIDS, T), F32),
        in_specs=[VMEM],
        out_specs=VMEM,
        compiler_params=params(4),
        name="square",
    )(streams_in)

    def along(value, axis, steps):
        size = lax.axis_size(axis)
        return lax.ppermute(value, axis, [(i, (i + steps) % size) for i in range(size)])

    messages = (along(fwd, "beam", 1), along(bwd, "beam", -1))
    r1, r2, r3 = [along(part, "tensor", k) for k in range(1, tens)]

    bc = bc_inputs[0].reshape(KIDS, T, 512)
    inc = jnp.transpose(unbiased_increments[0], (0, 2, 1))
    skip = jnp.repeat(skip_gain, 64, axis=1)
    taps_bc = conv_bc_weight[0]
    taps = conv_x_weight[0]
    *decays, grow, weight, last = pl.pallas_call(
        pre_kernel,
        out_shape=(
            shape((T, CD), F32),
            shape((T, CD), F32),
            shape((KIDS, HD, T), F32),
            shape((KIDS, HD, T), F32),
            shape((KIDS, HD, N), F32),
        ),
        in_specs=[SMEM] + [VMEM] * 3,
        out_specs=tuple([VMEM] * 5),
        compiler_params=params(10),
        cost_estimate=cost(200_000_000, 5_000_000, 1_000_000),
        name="pre",
    )(lengths, inc, a_log, dt_bias)

    early = ()
    kept = []
    for c in range(KIDS):
        out_dims = ((T, CD), (1, T)) if c == 0 else ((KIDS, T, CD), (KIDS, T))
        result = pl.pallas_call(
            functools.partial(mid_kernel, c),
            out_shape=(
                shape(out_dims[0], BF16),
                shape(out_dims[1], F32),
                shape((c + 1, 3, 2, 256), BF16),
                shape((T, CD), BF16),
                shape((T, CD), BF16),
                shape((T, 256), BF16),
            ),
            in_specs=[SMEM] + [VMEM] * (14 + len(early)),
            out_specs=tuple([VMEM] * 6),
            scratch_shapes=[pltpu.VMEM((72, 512), F32), pltpu.VMEM((72, CD), F32)],
            compiler_params=params(12),
            cost_estimate=cost(100_000_000, 3_000_000, 500_000),
            name="mid%d" % c,
        )(
            lengths,
            messages[c],
            bc,
            taps_bc,
            streams_in,
            part,
            r1,
            r2,
            r3,
            input_norm_gain,
            taps,
            skip,
            out_gain,
            decays[c],
            grow,
            *early,
        )
        early = result[:3]
        kept.append(result[3:])
    mid, mid_part, bc_out = early
    mixes, reads, b_mats = zip(*kept)

    moved = lax.ppermute(mid, "section", [(0, 1), (1, 0)])
    q1, q2, q3 = [
        lax.ppermute(
            mid_part, ("section", "tensor"), [(i, tens + (i + k) % tens) for i in range(tens)]
        )
        for k in range(1, tens)
    ]

    others = pl.pallas_call(
        others_kernel,
        out_shape=shape((KIDS, T), F32),
        in_specs=[SMEM] + [VMEM] * 6,
        out_specs=VMEM,
        compiler_params=params(4),
        cost_estimate=cost(10_000_000_000, 100_000_000, 0),
        name="others",
    )(section, r1, r2, r3, q1, q2, q3)

    out, new, x_out = pl.pallas_call(
        last_kernel,
        out_shape=(
            shape((KIDS, T, CD), BF16),
            shape((KIDS, CD, N), BF16),
            shape((3, KIDS, CD), BF16),
        ),
        in_specs=[SMEM] * 2 + [VMEM] * 15 + [HBM] * 2,
        out_specs=(HBM, HBM, VMEM),
        scratch_shapes=[
            pltpu.VMEM((72, CD), F32),
            pltpu.VMEM((KIDS, CD + 64, N), BF16),
            pltpu.VMEM((KIDS, T, CD), BF16),
            pltpu.VMEM((KIDS, CD, N), BF16),
            pltpu.SemaphoreType.DMA((3, KIDS)),
        ],
        compiler_params=params(14),
        cost_estimate=cost(200_000_000, 5_000_000, 1_000_000),
        name="last",
    )(
        section,
        lengths,
        others,
        input_norm_gain,
        taps,
        skip,
        out_gain,
        *b_mats,
        last,
        streams_in,
        moved,
        weight,
        *mixes,
        *reads,
        *messages,
    )
    return (
        out[None],
        new.reshape(1, KIDS, HD, 64, N),
        jnp.transpose(x_out, (1, 0, 2))[None],
        bc_out[None],
    )


def solution(mesh):
    placed = (
        P("beam", None, "tensor"),
        P("section", "beam", "tensor", None, None),
        P("section", "beam", None, "tensor"),
        P("section", "beam", None, None, "tensor"),
        P("section", "beam", None, None, "tensor"),
        P("section", "beam", None, "tensor"),
        P(),
        P("beam"),
        P("section", "tensor"),
        P("section", None, "tensor"),
        P("section", None, None, "tensor"),
        P("section", "tensor"),
        P("section", "tensor"),
        P("section", "tensor"),
        P("section", "tensor"),
    )
    return jax.shard_map(
        on_device,
        mesh=mesh,
        in_specs=placed,
        out_specs=(
            P("section", "beam", None, "tensor"),
            P("section", "beam", "tensor", None, None),
            P("section", "beam", None, "tensor"),
            P("section", "beam", None, None, "tensor"),
        ),
        check_vma=False,
    )
```

```python
import functools

import jax
import jax.numpy as jnp
from jax import lax
from jax.experimental import pallas as pl
from jax.experimental.pallas import tpu as pltpu
from jax.sharding import PartitionSpec as P

CH = 8192
EPS = 1e-05
KIDS = 2
T = 64
CD = 2048
HD = 32
N = 128
W = 256
GC = 1024
F32 = jnp.float32
BF16 = jnp.bfloat16
HIGHEST = lax.Precision.HIGHEST
VMEM = pl.BlockSpec(memory_space=pltpu.VMEM)
SMEM = pl.BlockSpec(memory_space=pltpu.SMEM)
HBM = pl.BlockSpec(memory_space=pl.ANY)
BIG = 60


def iota(shape, dim):
    return lax.broadcasted_iota(jnp.int32, shape, dim)


def as_row(col):
    size = col.shape[0]
    keep = iota((size, size), 0) == iota((size, size), 1)
    return jnp.sum(jnp.where(keep, col, 0.0), axis=0, keepdims=True)


def as_col(row):
    size = row.shape[1]
    keep = iota((size, size), 0) == iota((size, size), 1)
    return jnp.sum(jnp.where(keep, row, 0.0), axis=1, keepdims=True)


def silu(v):
    return 0.5 * v * (1.0 + jnp.tanh(0.5 * v))


def dot(a, b, dims, precision=None):
    return lax.dot_general(
        a, b, (dims, ((), ())), precision=precision, preferred_element_type=F32
    )


def three_parts(v):
    high = v.astype(BF16)
    rest = v - high.astype(F32)
    mid = rest.astype(BF16)
    low = (rest - mid.astype(F32)).astype(BF16)
    return [high, mid, low]


def pick_kernel(
    parents_in_ref,
    conv_x_in_ref,
    conv_bc_in_ref,
    state_in_ref,
    one_ref,
    two_ref,
    parents_ref,
    conv_x_ref,
    conv_bc_ref,
    state_ref,
    rows_ref,
    sems,
    out_sems,
):
    get_parents = pltpu.make_async_copy(parents_in_ref, parents_ref, sems.at[0])
    get_states = [
        pltpu.make_async_copy(state_in_ref.at[i], state_ref.at[i], sems.at[1 + i])
        for i in range(KIDS)
    ]
    get_x = pltpu.make_async_copy(conv_x_in_ref, conv_x_ref, sems.at[3])
    get_bc = pltpu.make_async_copy(conv_bc_in_ref, conv_bc_ref, sems.at[4])
    for copy in (get_parents, *get_states, get_x, get_bc):
        copy.start()
    peers = lax.axis_size("beam")
    me = lax.axis_index("beam")
    get_parents.wait()
    picks = (
        lax.rem(parents_ref[KIDS * lax.rem(me + 1, peers)], KIDS),
        lax.rem(parents_ref[KIDS * lax.rem(me + peers - 1, peers) + 1], KIDS),
    )
    outs = (one_ref, two_ref)
    for copy in get_states:
        copy.wait()
    puts = []
    for i in range(2):
        puts.append(
            pltpu.make_async_copy(state_ref.at[picks[i]], outs[i].at[:CD], out_sems.at[0, i])
        )
        puts[-1].start()
    get_x.wait()
    get_bc.wait()
    for i in range(2):
        low = picks[i] == 0
        pieces = []
        for k in range(3):
            both = conv_x_ref[k].astype(F32)
            row = jnp.where(low, both[0:1], both[1:2])
            pieces += [row[:, N * j : N * (j + 1)] for j in range(CD // N)]
        for k in range(3):
            both = conv_bc_ref[picks[i], k].astype(F32)
            pieces += [both[p : p + 1, N * j : N * (j + 1)] for p in range(2) for j in range(2)]
        pieces.append(jnp.zeros((4, N), F32))
        rows_ref[i] = jnp.concatenate(pieces, axis=0).astype(BF16)
        puts.append(pltpu.make_async_copy(rows_ref.at[i], outs[i].at[CD:], out_sems.at[1, i]))
        puts[-1].start()
    for copy in puts:
        copy.wait()


def square_kernel(stream_ref, part_ref):
    for c in range(KIDS):
        s = stream_ref[c].astype(F32)
        part_ref[c : c + 1, :] = as_row(jnp.sum(s * s, axis=1, keepdims=True))


def lay_rows(rows, past_ref):
    for k in range(3):
        for j in range(CD // N):
            at = 16 * k + j
            past_ref[5 + k : 6 + k, N * j : N * (j + 1)] = rows[at : at + 1, :]


def delayed(value, past, steps):
    rolled = pltpu.roll(value, steps, 0)
    head = jnp.where(iota(past.shape, 0) < steps, pltpu.roll(past, steps, 0), rolled[:8])
    return jnp.concatenate([head, rolled[8:]], axis=0)


def scaled_x(s, at, scale, gain_ref):
    return (s * scale * gain_ref[:, at]).astype(BF16).astype(F32)


def fresh_x(x_in, at, taps_ref, valid, past_ref):
    acc = taps_ref[3:4, at] * x_in
    for k in range(1, 4):
        acc = acc + taps_ref[3 - k : 4 - k, at] * delayed(x_in, past_ref[:8, at], k)
    return silu(acc) * valid


def head_masks():
    lane = iota((T, W), 1) // 64
    return [jnp.where(lane == j, 1.0, 0.0).astype(BF16) for j in range(4)]


def intra(mix, x, masks):
    xb = x.astype(BF16)
    return dot(mix, jnp.concatenate([xb * mask for mask in masks], axis=0), ((1,), (0,)))


def head_offsets():
    return iota((3 * HD, W), 0) % HD - iota((3 * HD, W), 1) // 64


def spread(parts, offsets, q):
    onehot = jnp.where(offsets == 4 * q, 1.0, 0.0).astype(BF16)
    return dot(parts, onehot, ((1,), (0,)))


def halves(v):
    return v[:, :N] + v[:, N:]


def fresh_bc(rows, bc, taps_ref, pbc_ref):
    for k in range(3):
        for j in range(4):
            at = 48 + 4 * k + j
            pbc_ref[5 + k : 6 + k, N * j : N * (j + 1)] = rows[at : at + 1, :]
    pbc_ref[8:72, :] = bc.astype(F32)
    acc = 0.0
    for k in range(4):
        taps = jnp.concatenate([taps_ref[k, 0:1, :], taps_ref[k, 1:2, :]], axis=1)
        acc = acc + taps * pbc_ref[5 + k : 69 + k, :]
    return silu(acc)


def valid_col(length):
    return jnp.where(iota((T, 1), 0) < length, 1.0, 0.0)


def spread_heads(compact):
    onehot = jnp.where(iota((HD, CD), 0) == iota((HD, CD), 1) // 64, 1.0, 0.0).astype(BF16)
    onehot = jnp.concatenate([onehot] * 3, axis=0)
    return dot(jnp.concatenate(three_parts(compact), axis=0), onehot, ((0,), (0,)))


def pre_kernel(
    len_ref, inc_ref, log_ref, bias_ref, decay0_ref, decay1_ref, grow_ref, weight_ref, last_ref
):
    rate = as_col(jnp.exp(log_ref[...]))
    bias = as_col(bias_ref[...])
    upper = jnp.where(iota((T, T), 0) <= iota((T, T), 1), 1.0, 0.0)
    diag = iota((T, CD), 1) % T == iota((T, CD), 0)
    causal = iota((T, CD), 0) >= iota((T, CD), 1) % T
    for c in range(KIDS):
        valid_row = jnp.where(iota((1, T), 1) < len_ref[c], 1.0, 0.0)
        raw = inc_ref[c] + bias
        dt = (jnp.maximum(raw, 0.0) + jnp.log1p(jnp.exp(-jnp.abs(raw)))) * valid_row
        cum = dot(-dt * rate, upper, ((1,), (0,)), HIGHEST)
        final = cum[:, T - 1 : T]
        last_ref[c] = jnp.broadcast_to(jnp.exp(final), (HD, N))
        for ref, value in ((grow_ref, jnp.exp(cum)), (weight_ref, jnp.exp(final - cum) * dt)):
            parts = jnp.concatenate([part.astype(F32) for part in three_parts(value)], axis=0)
            ref[c] = parts.T.astype(BF16)
        edt = spread_heads(dt)
        ecum = spread_heads(cum)
        row_dt = jnp.sum(jnp.where(diag, edt, 0.0), axis=0, keepdims=True)
        row_cum = jnp.sum(jnp.where(diag, ecum, 0.0), axis=0, keepdims=True)
        gap = jnp.exp(jnp.minimum(ecum - row_cum, 0.0))
        (decay0_ref, decay1_ref)[c][...] = jnp.where(causal, gap * row_dt, 0.0)


def mid_kernel(
    c,
    sec_ref,
    len_ref,
    message_ref,
    bc_ref,
    taps_bc_ref,
    stream_ref,
    totals_ref,
    gain_in_ref,
    taps_ref,
    skip_ref,
    gain_ref,
    decay_ref,
    grow_ref,
    *refs,
):
    if c == 1:
        early_ref, early_part_ref = refs[:2]
        refs = refs[2:]
    out_ref, part_ref, mix_ref, read_ref, b_ref, pbc_ref, past_ref, y_ref = refs
    rows = message_ref[CD:, :].astype(F32)
    bc = fresh_bc(rows, bc_ref[c], taps_bc_ref, pbc_ref)
    b_ref[...] = bc[:, :W].astype(BF16)
    inner = []
    for g in range(2):
        bg = bc[:, N * g : N * (g + 1)]
        cg = bc[:, W + N * g : W + N * (g + 1)]
        inner.append(dot(cg, jnp.concatenate([bg] * 4, axis=0), ((1,), (1,)), HIGHEST))
    cb = bc[:, W:].astype(BF16)
    valid = valid_col(len_ref[c])
    scale = lax.rsqrt(as_col(totals_ref[c : c + 1]) / CH + EPS)
    lay_rows(rows, past_ref)
    masks = head_masks()
    offsets = head_offsets()
    sums = [0.0, 0.0]
    for q in range(CD // W):
        at = slice(W * q, W * (q + 1))
        g = q // 4
        s = stream_ref[c, :, at].astype(F32)
        x = fresh_x(scaled_x(s, at, scale, gain_in_ref), at, taps_ref, valid, past_ref)
        mix = (decay_ref[:, at] * inner[g]).astype(BF16)
        mix_ref[:, at] = mix
        read = dot(cb[:, N * g : N * (g + 1)], message_ref[at, :], ((1,), (1,)))
        read = read * spread(grow_ref[c], offsets, q)
        read_ref[:, at] = read.astype(BF16)
        y = intra(mix, x, masks) + skip_ref[:, at] * x + read
        y_ref[:, at] = y
        sums[g] = sums[g] + halves(y * y)
    norm = [
        lax.rsqrt(jnp.sum(v, axis=1, keepdims=True) * (1.0 / GC) + EPS) * valid for v in sums
    ]
    squares = 0.0
    first = sec_ref[0] == 0
    for q in range(CD // W):
        at = slice(W * q, W * (q + 1))
        z = y_ref[:, at] * norm[q // 4] * gain_ref[:, at]
        out = (stream_ref[c, :, at].astype(F32) + jnp.where(first, z, 0.0)).astype(BF16)
        s = out.astype(F32)
        squares = squares + halves(s * s)
        if c == 0:
            out_ref[:, at] = out
        else:
            out_ref[1, :, at] = out
            out_ref[0, :, at] = early_ref[:, at]
    part = as_row(jnp.sum(squares, axis=1, keepdims=True))
    if c == 0:
        part_ref[...] = part
    else:
        part_ref[0:1, :] = early_part_ref[...]
        part_ref[1:2, :] = part


def totals_kernel(p_ref, r1_ref, r2_ref, r3_ref, totals_ref, rest_ref):
    rest = r1_ref[...] + r2_ref[...] + r3_ref[...]
    rest_ref[...] = rest
    totals_ref[...] = p_ref[...] + rest


def others_kernel(sec_ref, rest_ref, q1_ref, q2_ref, q3_ref, others_ref):
    others_ref[...] = jnp.where(
        sec_ref[0] == 0, rest_ref[...], q1_ref[...] + q2_ref[...] + q3_ref[...]
    )


def last_kernel(
    len_ref,
    others_ref,
    gain_in_ref,
    taps_ref,
    skip_ref,
    gain_ref,
    bc_ref,
    b0_ref,
    b1_ref,
    last_ref,
    moved_ref,
    weight_ref,
    mix0_ref,
    mix1_ref,
    read0_ref,
    read1_ref,
    message0_in_ref,
    message1_in_ref,
    out_to_ref,
    new_to_ref,
    x_to_ref,
    bc_to_ref,
    px_ref,
    y_ref,
    xw_ref,
    pbc_ref,
    message_ref,
    out_ref,
    new_ref,
    x_out_ref,
    bc_out_ref,
    sems,
    new_sems,
):
    gets = [
        pltpu.make_async_copy(
            (message0_in_ref, message1_in_ref)[c], message_ref.at[c], sems.at[c]
        )
        for c in range(KIDS)
    ]
    for copy in gets:
        copy.start()
    puts = []

    def send(source, target, sem):
        puts.append(pltpu.make_async_copy(source, target, sem))
        puts[-1].start()

    masks = head_masks()
    offsets = head_offsets()
    chunks = [slice(W * q, W * (q + 1)) for q in range(CD // W)]
    tails = []
    for c in range(KIDS):
        length = len_ref[c]
        valid = valid_col(length)
        squares = 0.0
        for at in chunks:
            s = moved_ref[c, :, at].astype(F32)
            squares = squares + halves(s * s)
        total = jnp.sum(squares, axis=1, keepdims=True) + as_col(others_ref[c : c + 1])
        scale = lax.rsqrt(total / CH + EPS)
        gets[c].wait()
        rows = message_ref[c, CD:, :].astype(F32)
        lay_rows(rows, px_ref)
        for k in range(3):
            for j in range(4):
                at = 48 + 4 * k + j
                pbc_ref[5 + k : 6 + k, N * j : N * (j + 1)] = rows[at : at + 1, :]
        pbc_ref[8:72, :] = bc_ref[c].astype(F32)
        for k in range(3):
            row = pbc_ref[pl.ds(5 + length + k, 1), :]
            bc_out_ref[c, k] = jnp.concatenate([row[:, :W], row[:, W:]], axis=0).astype(BF16)
        sums = [0.0, 0.0]
        for q, at in enumerate(chunks):
            x_in = scaled_x(moved_ref[c, :, at].astype(F32), at, scale, gain_in_ref)
            px_ref[8:72, at] = x_in
            x = fresh_x(x_in, at, taps_ref, valid, px_ref)
            xw_ref[:, at] = (x * spread(weight_ref[c], offsets, q)).astype(BF16)
            y = intra((mix0_ref, mix1_ref)[c][:, at], x, masks) + skip_ref[:, at] * x
            y = y + (read0_ref, read1_ref)[c][:, at].astype(F32)
            y_ref[:, at] = y
            sums[q // 4] = sums[q // 4] + halves(y * y)
        tails.append([px_ref[pl.ds(5 + length + k, 1), :] for k in range(3)])
        if c == KIDS - 1:
            for k in range(3):
                x_out_ref[k] = jnp.concatenate([tails[0][k], tails[1][k]], axis=0).astype(BF16)
            send(x_out_ref, x_to_ref, sems.at[2])
            send(bc_out_ref, bc_to_ref, sems.at[3])
        norm = [
            lax.rsqrt(jnp.sum(v, axis=1, keepdims=True) * (1.0 / GC) + EPS) * valid for v in sums
        ]
        for q, at in enumerate(chunks):
            z = y_ref[:, at] * norm[q // 4] * gain_ref[:, at]
            out_ref[c, :, at] = (moved_ref[c, :, at].astype(F32) + z).astype(BF16)
        send(out_ref.at[c], out_to_ref.at[c], sems.at[4 + c])
        for q, at in enumerate(chunks):
            g = q // 4
            fresh = dot(xw_ref[:, at], (b0_ref, b1_ref)[c][:, N * g : N * (g + 1)], ((0,), (0,)))
            for j in range(4):
                rows_at = slice(W * q + 64 * j, W * q + 64 * (j + 1))
                h = 4 * q + j
                new_ref[c, rows_at, :] = (
                    last_ref[c, h : h + 1, :] * message_ref[c, rows_at, :].astype(F32)
                    + fresh[64 * j : 64 * (j + 1)]
                ).astype(BF16)
            if q % 4 == 3:
                half = pl.ds(GC * g, GC)
                send(new_ref.at[c, half], new_to_ref.at[c, half], new_sems.at[c, g])
    for copy in puts:
        copy.wait()


def shape(dims, kind):
    return jax.ShapeDtypeStruct(dims, kind)


def params(mib):
    return pltpu.CompilerParams(vmem_limit_bytes=mib * 2**20)


def cost(flops, moved, exps=0):
    return pl.CostEstimate(flops=flops, bytes_accessed=moved, transcendentals=exps)


def on_device(
    streams_in,
    beam_state_cache,
    conv_x_cache,
    conv_bc_cache,
    bc_inputs,
    unbiased_increments,
    parents,
    lengths,
    input_norm_gain,
    conv_x_weight,
    conv_bc_weight,
    a_log,
    dt_bias,
    skip_gain,
    out_gain,
):
    tens = lax.axis_size("tensor")
    peers = lax.axis_size("beam")
    section = lax.axis_index("section").astype(jnp.int32)[None]
    message = shape((CD + 64, N), BF16)
    fwd, bwd = pl.pallas_call(
        pick_kernel,
        out_shape=(message, message),
        in_specs=[HBM] * 4,
        out_specs=(HBM, HBM),
        scratch_shapes=[
            pltpu.SMEM(parents.shape, jnp.int32),
            pltpu.VMEM((3, KIDS, CD), BF16),
            pltpu.VMEM((KIDS, 3, 2, 256), BF16),
            pltpu.VMEM((KIDS, CD, N), BF16),
            pltpu.VMEM((2, 64, N), BF16),
            pltpu.SemaphoreType.DMA((5,)),
            pltpu.SemaphoreType.DMA((2, 2)),
        ],
        compiler_params=params(BIG),
        name="pick",
    )(
        parents,
        jnp.transpose(conv_x_cache[0], (1, 0, 2)),
        conv_bc_cache[0],
        beam_state_cache[0].reshape(KIDS, CD, N),
    )
    part = pl.pallas_call(
        square_kernel,
        out_shape=shape((KIDS, T), F32),
        in_specs=[VMEM],
        out_specs=VMEM,
        compiler_params=params(4),
        name="square",
    )(streams_in)

    def along(value, axis, steps):
        size = lax.axis_size(axis)
        return lax.ppermute(value, axis, [(i, (i + steps) % size) for i in range(size)])

    messages = (along(fwd, "beam", 1), along(bwd, "beam", -1))
    r1, r2, r3 = [along(part, "tensor", k) for k in range(1, tens)]

    bc = bc_inputs[0].reshape(KIDS, T, 512)
    inc = jnp.transpose(unbiased_increments[0], (0, 2, 1))
    skip = jnp.repeat(skip_gain, 64, axis=1)
    taps_bc = conv_bc_weight[0]
    taps = conv_x_weight[0]
    *decays, grow, weight, last = pl.pallas_call(
        pre_kernel,
        out_shape=(
            shape((T, CD), F32),
            shape((T, CD), F32),
            shape((KIDS, T, 3 * HD), BF16),
            shape((KIDS, T, 3 * HD), BF16),
            shape((KIDS, HD, N), F32),
        ),
        in_specs=[SMEM] + [VMEM] * 3,
        out_specs=tuple([VMEM] * 5),
        compiler_params=params(10),
        cost_estimate=cost(200_000_000, 5_000_000, 1_000_000),
        name="pre",
    )(lengths, inc, a_log, dt_bias)

    totals, rest = pl.pallas_call(
        totals_kernel,
        out_shape=(shape((KIDS, T), F32), shape((KIDS, T), F32)),
        in_specs=[VMEM] * 4,
        out_specs=(VMEM, VMEM),
        compiler_params=params(4),
        name="totals",
    )(part, r1, r2, r3)

    early = ()
    kept = []
    for c in range(KIDS):
        out_dims = ((T, CD), (1, T)) if c == 0 else ((KIDS, T, CD), (KIDS, T))
        result = pl.pallas_call(
            functools.partial(mid_kernel, c),
            out_shape=(
                shape(out_dims[0], BF16),
                shape(out_dims[1], F32),
                shape((T, CD), BF16),
                shape((T, CD), BF16),
                shape((T, 256), BF16),
            ),
            in_specs=[SMEM] * 2 + [VMEM] * (11 + len(early)),
            out_specs=tuple([VMEM] * 5),
            scratch_shapes=[
                pltpu.VMEM((72, 512), F32),
                pltpu.VMEM((8, CD), F32),
                pltpu.VMEM((T, CD), F32),
            ],
            compiler_params=params(12),
            cost_estimate=cost(100_000_000, 3_000_000, 500_000),
            name="mid%d" % c,
        )(
            section,
            lengths,
            messages[c],
            bc,
            taps_bc,
            streams_in,
            totals,
            input_norm_gain,
            taps,
            skip,
            out_gain,
            decays[c],
            grow,
            *early,
        )
        early = result[:2]
        kept.append(result[2:])
    mid, mid_part = early
    mixes, reads, b_mats = zip(*kept)

    moved = lax.ppermute(mid, "section", [(0, 1), (1, 0)])
    q1, q2, q3 = [
        lax.ppermute(
            mid_part, ("section", "tensor"), [(i, tens + (i + k) % tens) for i in range(tens)]
        )
        for k in range(1, tens)
    ]

    others = pl.pallas_call(
        others_kernel,
        out_shape=shape((KIDS, T), F32),
        in_specs=[SMEM] + [VMEM] * 4,
        out_specs=VMEM,
        compiler_params=params(4),
        cost_estimate=cost(10_000_000_000, 100_000_000, 0),
        name="others",
    )(section, rest, q1, q2, q3)

    out, new, x_out, bc_out = pl.pallas_call(
        last_kernel,
        out_shape=(
            shape((KIDS, T, CD), BF16),
            shape((KIDS, CD, N), BF16),
            shape((3, KIDS, CD), BF16),
            shape((KIDS, 3, 2, W), BF16),
        ),
        in_specs=[SMEM] + [VMEM] * 15 + [HBM] * 2,
        out_specs=(HBM, HBM, HBM, HBM),
        scratch_shapes=[
            pltpu.VMEM((72, CD), F32),
            pltpu.VMEM((T, CD), F32),
            pltpu.VMEM((T, CD), BF16),
            pltpu.VMEM((72, 512), F32),
            pltpu.VMEM((KIDS, CD + 64, N), BF16),
            pltpu.VMEM((KIDS, T, CD), BF16),
            pltpu.VMEM((KIDS, CD, N), BF16),
            pltpu.VMEM((3, KIDS, CD), BF16),
            pltpu.VMEM((KIDS, 3, 2, W), BF16),
            pltpu.SemaphoreType.DMA((6,)),
            pltpu.SemaphoreType.DMA((KIDS, 2)),
        ],
        compiler_params=params(14),
        cost_estimate=cost(200_000_000, 5_000_000, 1_000_000),
        name="last",
    )(
        lengths,
        others,
        input_norm_gain,
        taps,
        skip,
        out_gain,
        bc,
        *b_mats,
        last,
        moved,
        weight,
        *mixes,
        *reads,
        *messages,
    )
    return (
        out[None],
        new.reshape(1, KIDS, HD, 64, N),
        jnp.transpose(x_out, (1, 0, 2))[None],
        bc_out[None],
    )


def solution(mesh):
    placed = (
        P("beam", None, "tensor"),
        P("section", "beam", "tensor", None, None),
        P("section", "beam", None, "tensor"),
        P("section", "beam", None, None, "tensor"),
        P("section", "beam", None, None, "tensor"),
        P("section", "beam", None, "tensor"),
        P(),
        P("beam"),
        P("section", "tensor"),
        P("section", None, "tensor"),
        P("section", None, None, "tensor"),
        P("section", "tensor"),
        P("section", "tensor"),
        P("section", "tensor"),
        P("section", "tensor"),
    )
    return jax.shard_map(
        on_device,
        mesh=mesh,
        in_specs=placed,
        out_specs=(
            P("section", "beam", None, "tensor"),
            P("section", "beam", "tensor", None, None),
            P("section", "beam", None, "tensor"),
            P("section", "beam", None, None, "tensor"),
        ),
        check_vma=False,
    )
```

```python
import functools

import jax
import jax.numpy as jnp
from jax import lax
from jax.experimental import pallas as pl
from jax.experimental.pallas import tpu as pltpu
from jax.sharding import PartitionSpec as P

CH = 8192
EPS = 1e-05
KIDS = 2
T = 64
CD = 2048
HD = 32
N = 128
W = 256
GC = 1024
F32 = jnp.float32
BF16 = jnp.bfloat16
HIGHEST = lax.Precision.HIGHEST
VMEM = pl.BlockSpec(memory_space=pltpu.VMEM)
SMEM = pl.BlockSpec(memory_space=pltpu.SMEM)
HBM = pl.BlockSpec(memory_space=pl.ANY)
BIG = 60
PARTS = 4
LATE = 1


def iota(shape, dim):
    return lax.broadcasted_iota(jnp.int32, shape, dim)


def as_row(col):
    size = col.shape[0]
    keep = iota((size, size), 0) == iota((size, size), 1)
    return jnp.sum(jnp.where(keep, col, 0.0), axis=0, keepdims=True)


def as_col(row):
    size = row.shape[1]
    keep = iota((size, size), 0) == iota((size, size), 1)
    return jnp.sum(jnp.where(keep, row, 0.0), axis=1, keepdims=True)


def silu(v):
    return 0.5 * v * (1.0 + jnp.tanh(0.5 * v))


def dot(a, b, dims, precision=None):
    return lax.dot_general(
        a, b, (dims, ((), ())), precision=precision, preferred_element_type=F32
    )


def three_parts(v):
    high = v.astype(BF16)
    rest = v - high.astype(F32)
    mid = rest.astype(BF16)
    low = (rest - mid.astype(F32)).astype(BF16)
    return [high, mid, low]


def pick_kernel(
    parents_in_ref,
    conv_x_in_ref,
    conv_bc_in_ref,
    state_in_ref,
    one_ref,
    two_ref,
    parents_ref,
    conv_x_ref,
    conv_bc_ref,
    state_ref,
    rows_ref,
    sems,
    out_sems,
):
    get_parents = pltpu.make_async_copy(parents_in_ref, parents_ref, sems.at[0])
    parts = [pl.ds(CD // PARTS * j, CD // PARTS) for j in range(PARTS)]
    get_states = [
        pltpu.make_async_copy(state_in_ref.at[i, at], state_ref.at[i, at], sems.at[3 + KIDS * j + i])
        for j, at in enumerate(parts)
        for i in range(KIDS)
    ]
    get_x = pltpu.make_async_copy(conv_x_in_ref, conv_x_ref, sems.at[1])
    get_bc = pltpu.make_async_copy(conv_bc_in_ref, conv_bc_ref, sems.at[2])
    for copy in (get_parents, get_x, get_bc, *get_states):
        copy.start()
    peers = lax.axis_size("beam")
    me = lax.axis_index("beam")
    get_parents.wait()
    picks = (
        lax.rem(parents_ref[KIDS * lax.rem(me + 1, peers)], KIDS),
        lax.rem(parents_ref[KIDS * lax.rem(me + peers - 1, peers) + 1], KIDS),
    )
    outs = (one_ref, two_ref)
    get_x.wait()
    get_bc.wait()
    puts = []
    for i in range(2):
        low = picks[i] == 0
        pieces = []
        for k in range(3):
            both = conv_x_ref[k].astype(F32)
            row = jnp.where(low, both[0:1], both[1:2])
            pieces += [row[:, N * j : N * (j + 1)] for j in range(CD // N)]
        for k in range(3):
            both = conv_bc_ref[picks[i], k].astype(F32)
            pieces += [both[p : p + 1, N * j : N * (j + 1)] for p in range(2) for j in range(2)]
        pieces.append(jnp.zeros((4, N), F32))
        rows_ref[i] = jnp.concatenate(pieces, axis=0).astype(BF16)
        puts.append(pltpu.make_async_copy(rows_ref.at[i], outs[i].at[CD:], out_sems.at[i, PARTS]))
        puts[-1].start()
    for j, at in enumerate(parts):
        for i in range(KIDS):
            get_states[KIDS * j + i].wait()
        for i in range(2):
            puts.append(
                pltpu.make_async_copy(
                    state_ref.at[picks[i], at], outs[i].at[at], out_sems.at[i, j]
                )
            )
            puts[-1].start()
    for copy in puts:
        copy.wait()


def square_kernel(stream_ref, part_ref):
    for c in range(KIDS):
        s = stream_ref[c].astype(F32)
        part_ref[c : c + 1, :] = as_row(jnp.sum(s * s, axis=1, keepdims=True))


def lay_rows(rows, past_ref):
    for k in range(3):
        for j in range(CD // N):
            at = 16 * k + j
            past_ref[5 + k : 6 + k, N * j : N * (j + 1)] = rows[at : at + 1, :]


def delayed(value, past, steps):
    rolled = pltpu.roll(value, steps, 0)
    head = jnp.where(iota(past.shape, 0) < steps, pltpu.roll(past, steps, 0), rolled[:8])
    return jnp.concatenate([head, rolled[8:]], axis=0)


def scaled_x(s, at, scale, gain_ref):
    return (s * scale * gain_ref[:, at]).astype(BF16).astype(F32)


def fresh_x(x_in, at, taps_ref, valid, past_ref):
    acc = taps_ref[3:4, at] * x_in
    for k in range(1, 4):
        acc = acc + taps_ref[3 - k : 4 - k, at] * delayed(x_in, past_ref[:8, at], k)
    return silu(acc) * valid


def head_masks():
    lane = iota((T, W), 1) // 64
    return [jnp.where(lane == j, 1.0, 0.0).astype(BF16) for j in range(4)]


def intra(mix, x, masks):
    xb = x.astype(BF16)
    return dot(mix, jnp.concatenate([xb * mask for mask in masks], axis=0), ((1,), (0,)))


def head_offsets():
    return iota((3 * HD, W), 0) % HD - iota((3 * HD, W), 1) // 64


def spread(parts, offsets, q):
    onehot = jnp.where(offsets == 4 * q, 1.0, 0.0).astype(BF16)
    return dot(parts, onehot, ((1,), (0,)))


def halves(v):
    return v[:, :N] + v[:, N:]


def fresh_bc(rows, bc, taps_ref, pbc_ref):
    for k in range(3):
        for j in range(4):
            at = 48 + 4 * k + j
            pbc_ref[5 + k : 6 + k, N * j : N * (j + 1)] = rows[at : at + 1, :]
    pbc_ref[8:72, :] = bc.astype(F32)
    acc = 0.0
    for k in range(4):
        taps = jnp.concatenate([taps_ref[k, 0:1, :], taps_ref[k, 1:2, :]], axis=1)
        acc = acc + taps * pbc_ref[5 + k : 69 + k, :]
    return silu(acc)


def valid_col(length):
    return jnp.where(iota((T, 1), 0) < length, 1.0, 0.0)


def spread_heads(compact):
    onehot = jnp.where(iota((HD, CD), 0) == iota((HD, CD), 1) // 64, 1.0, 0.0).astype(BF16)
    onehot = jnp.concatenate([onehot] * 3, axis=0)
    return dot(jnp.concatenate(three_parts(compact), axis=0), onehot, ((0,), (0,)))


def pre_kernel(
    len_ref, inc_ref, log_ref, bias_ref, decay0_ref, decay1_ref, grow_ref, weight_ref, last_ref
):
    rate = as_col(jnp.exp(log_ref[...]))
    bias = as_col(bias_ref[...])
    upper = jnp.where(iota((T, T), 0) <= iota((T, T), 1), 1.0, 0.0)
    diag = iota((T, CD), 1) % T == iota((T, CD), 0)
    causal = iota((T, CD), 0) >= iota((T, CD), 1) % T
    for c in range(KIDS):
        valid_row = jnp.where(iota((1, T), 1) < len_ref[c], 1.0, 0.0)
        raw = inc_ref[c] + bias
        dt = (jnp.maximum(raw, 0.0) + jnp.log1p(jnp.exp(-jnp.abs(raw)))) * valid_row
        cum = dot(-dt * rate, upper, ((1,), (0,)), HIGHEST)
        final = cum[:, T - 1 : T]
        last_ref[c] = jnp.broadcast_to(jnp.exp(final), (HD, N))
        for ref, value in ((grow_ref, jnp.exp(cum)), (weight_ref, jnp.exp(final - cum) * dt)):
            parts = jnp.concatenate([part.astype(F32) for part in three_parts(value)], axis=0)
            ref[c] = parts.T.astype(BF16)
        edt = spread_heads(dt)
        ecum = spread_heads(cum)
        row_dt = jnp.sum(jnp.where(diag, edt, 0.0), axis=0, keepdims=True)
        row_cum = jnp.sum(jnp.where(diag, ecum, 0.0), axis=0, keepdims=True)
        gap = jnp.exp(jnp.minimum(ecum - row_cum, 0.0))
        (decay0_ref, decay1_ref)[c][...] = jnp.where(causal, gap * row_dt, 0.0)


def mid_kernel(
    c,
    sec_ref,
    len_ref,
    message_ref,
    bc_ref,
    taps_bc_ref,
    stream_ref,
    totals_ref,
    gain_in_ref,
    taps_ref,
    skip_ref,
    gain_ref,
    decay_ref,
    grow_ref,
    *refs,
):
    if c == LATE:
        early_ref, early_part_ref = refs[:2]
        refs = refs[2:]
    out_ref, part_ref, mix_ref, read_ref, b_ref, pbc_ref, past_ref, y_ref = refs
    rows = message_ref[CD:, :].astype(F32)
    bc = fresh_bc(rows, bc_ref[c], taps_bc_ref, pbc_ref)
    b_ref[...] = bc[:, :W].astype(BF16)
    inner = []
    for g in range(2):
        bg = bc[:, N * g : N * (g + 1)]
        cg = bc[:, W + N * g : W + N * (g + 1)]
        inner.append(dot(cg, jnp.concatenate([bg] * 4, axis=0), ((1,), (1,)), HIGHEST))
    cb = bc[:, W:].astype(BF16)
    valid = valid_col(len_ref[c])
    scale = lax.rsqrt(as_col(totals_ref[c : c + 1]) / CH + EPS)
    lay_rows(rows, past_ref)
    masks = head_masks()
    offsets = head_offsets()
    sums = [0.0, 0.0]
    for q in range(CD // W):
        at = slice(W * q, W * (q + 1))
        g = q // 4
        s = stream_ref[c, :, at].astype(F32)
        x = fresh_x(scaled_x(s, at, scale, gain_in_ref), at, taps_ref, valid, past_ref)
        mix = (decay_ref[:, at] * inner[g]).astype(BF16)
        mix_ref[:, at] = mix
        read = dot(cb[:, N * g : N * (g + 1)], message_ref[at, :], ((1,), (1,)))
        read = read * spread(grow_ref[c], offsets, q)
        read_ref[:, at] = read.astype(BF16)
        y = intra(mix, x, masks) + skip_ref[:, at] * x + read
        y_ref[:, at] = y
        sums[g] = sums[g] + halves(y * y)
    norm = [
        lax.rsqrt(jnp.sum(v, axis=1, keepdims=True) * (1.0 / GC) + EPS) * valid for v in sums
    ]
    squares = 0.0
    first = sec_ref[0] == 0
    for q in range(CD // W):
        at = slice(W * q, W * (q + 1))
        z = y_ref[:, at] * norm[q // 4] * gain_ref[:, at]
        out = (stream_ref[c, :, at].astype(F32) + jnp.where(first, z, 0.0)).astype(BF16)
        s = out.astype(F32)
        squares = squares + halves(s * s)
        if c == LATE:
            out_ref[c, :, at] = out
            out_ref[1 - c, :, at] = early_ref[:, at]
        else:
            out_ref[:, at] = out
    part = as_row(jnp.sum(squares, axis=1, keepdims=True))
    if c == LATE:
        part_ref[c : c + 1, :] = part
        part_ref[1 - c : 2 - c, :] = early_part_ref[...]
    else:
        part_ref[...] = part


def totals_kernel(p_ref, r1_ref, r2_ref, r3_ref, totals_ref):
    totals_ref[...] = p_ref[...] + r1_ref[...] + r2_ref[...] + r3_ref[...]


def others_kernel(q1_ref, q2_ref, q3_ref, others_ref):
    others_ref[...] = q1_ref[...] + q2_ref[...] + q3_ref[...]


def last_kernel(
    len_ref,
    others_ref,
    gain_in_ref,
    taps_ref,
    skip_ref,
    gain_ref,
    bc_ref,
    b0_ref,
    b1_ref,
    last_ref,
    moved_ref,
    weight_ref,
    mix0_ref,
    mix1_ref,
    read0_ref,
    read1_ref,
    message0_ref,
    message1_ref,
    out_to_ref,
    new_to_ref,
    x_to_ref,
    bc_to_ref,
    px_ref,
    y_ref,
    xw_ref,
    pbc_ref,
    out_ref,
    new_ref,
    x_out_ref,
    bc_out_ref,
    sems,
    new_sems,
):
    puts = []

    def send(source, target, sem):
        puts.append(pltpu.make_async_copy(source, target, sem))
        puts[-1].start()

    masks = head_masks()
    offsets = head_offsets()
    chunks = [slice(W * q, W * (q + 1)) for q in range(CD // W)]
    messages = (message0_ref, message1_ref)
    valids = [valid_col(len_ref[c]) for c in range(KIDS)]
    scales = []
    for c in range(KIDS):
        squares = 0.0
        for at in chunks:
            s = moved_ref[c, :, at].astype(F32)
            squares = squares + halves(s * s)
        total = jnp.sum(squares, axis=1, keepdims=True) + as_col(others_ref[c : c + 1])
        scales.append(lax.rsqrt(total / CH + EPS))
        rows = messages[c][CD:, :].astype(F32)
        lay_rows(rows, px_ref.at[c])
        for k in range(3):
            for j in range(4):
                at = 48 + 4 * k + j
                pbc_ref[c, 5 + k : 6 + k, N * j : N * (j + 1)] = rows[at : at + 1, :]
        pbc_ref[c, 8:72, :] = bc_ref[c].astype(F32)
    sums = [[0.0, 0.0] for _ in range(KIDS)]
    for q, at in enumerate(chunks):
        for c in range(KIDS):
            x_in = scaled_x(moved_ref[c, :, at].astype(F32), at, scales[c], gain_in_ref)
            px_ref[c, 8:72, at] = x_in
            x = fresh_x(x_in, at, taps_ref, valids[c], px_ref.at[c])
            xw_ref[c, :, at] = (x * spread(weight_ref[c], offsets, q)).astype(BF16)
            y = intra((mix0_ref, mix1_ref)[c][:, at], x, masks) + skip_ref[:, at] * x
            y = y + (read0_ref, read1_ref)[c][:, at].astype(F32)
            y_ref[c, :, at] = y
            sums[c][q // 4] = sums[c][q // 4] + halves(y * y)
    for c in range(KIDS):
        norm = [
            lax.rsqrt(jnp.sum(v, axis=1, keepdims=True) * (1.0 / GC) + EPS) * valids[c]
            for v in sums[c]
        ]
        for q, at in enumerate(chunks):
            z = y_ref[c, :, at] * norm[q // 4] * gain_ref[:, at]
            out_ref[c, :, at] = (moved_ref[c, :, at].astype(F32) + z).astype(BF16)
    for c in range(KIDS):
        send(out_ref.at[c], out_to_ref.at[c], sems.at[4 + c])
    for k in range(3):
        tails = [px_ref[c, pl.ds(5 + len_ref[c] + k, 1), :] for c in range(KIDS)]
        x_out_ref[k] = jnp.concatenate(tails, axis=0).astype(BF16)
        for c in range(KIDS):
            row = pbc_ref[c, pl.ds(5 + len_ref[c] + k, 1), :]
            bc_out_ref[c, k] = jnp.concatenate([row[:, :W], row[:, W:]], axis=0).astype(BF16)
    send(x_out_ref, x_to_ref, sems.at[2])
    send(bc_out_ref, bc_to_ref, sems.at[3])
    for g in range(2):
        for c in range(KIDS):
            for q in range(4 * g, 4 * g + 4):
                b = (b0_ref, b1_ref)[c][:, N * g : N * (g + 1)]
                fresh = dot(xw_ref[c, :, chunks[q]], b, ((0,), (0,)))
                for j in range(4):
                    rows_at = slice(W * q + 64 * j, W * q + 64 * (j + 1))
                    h = 4 * q + j
                    new_ref[c, rows_at, :] = (
                        last_ref[c, h : h + 1, :] * messages[c][rows_at, :].astype(F32)
                        + fresh[64 * j : 64 * (j + 1)]
                    ).astype(BF16)
            half = pl.ds(GC * g, GC)
            send(new_ref.at[c, half], new_to_ref.at[c, half], new_sems.at[c, g])
    for copy in puts:
        copy.wait()


def shape(dims, kind):
    return jax.ShapeDtypeStruct(dims, kind)


def params(mib):
    return pltpu.CompilerParams(vmem_limit_bytes=mib * 2**20)


def cost(flops, moved, exps=0):
    return pl.CostEstimate(flops=flops, bytes_accessed=moved, transcendentals=exps)


def on_device(
    streams_in,
    beam_state_cache,
    conv_x_cache,
    conv_bc_cache,
    bc_inputs,
    unbiased_increments,
    parents,
    lengths,
    input_norm_gain,
    conv_x_weight,
    conv_bc_weight,
    a_log,
    dt_bias,
    skip_gain,
    out_gain,
):
    tens = lax.axis_size("tensor")
    peers = lax.axis_size("beam")
    section = lax.axis_index("section").astype(jnp.int32)[None]
    message = shape((CD + 64, N), BF16)
    fwd, bwd = pl.pallas_call(
        pick_kernel,
        out_shape=(message, message),
        in_specs=[HBM] * 4,
        out_specs=(HBM, HBM),
        scratch_shapes=[
            pltpu.SMEM(parents.shape, jnp.int32),
            pltpu.VMEM((3, KIDS, CD), BF16),
            pltpu.VMEM((KIDS, 3, 2, 256), BF16),
            pltpu.VMEM((KIDS, CD, N), BF16),
            pltpu.VMEM((2, 64, N), BF16),
            pltpu.SemaphoreType.DMA((3 + KIDS * PARTS,)),
            pltpu.SemaphoreType.DMA((2, PARTS + 1)),
        ],
        compiler_params=params(BIG),
        name="pick",
    )(
        parents,
        jnp.transpose(conv_x_cache[0], (1, 0, 2)),
        conv_bc_cache[0],
        beam_state_cache[0].reshape(KIDS, CD, N),
    )
    part = pl.pallas_call(
        square_kernel,
        out_shape=shape((KIDS, T), F32),
        in_specs=[VMEM],
        out_specs=VMEM,
        compiler_params=params(4),
        name="square",
    )(streams_in)

    def along(value, axis, steps):
        size = lax.axis_size(axis)
        return lax.ppermute(value, axis, [(i, (i + steps) % size) for i in range(size)])

    messages = (along(fwd, "beam", 1), along(bwd, "beam", -1))
    r1, r2, r3 = [along(part, "tensor", k) for k in range(1, tens)]

    bc = bc_inputs[0].reshape(KIDS, T, 512)
    inc = jnp.transpose(unbiased_increments[0], (0, 2, 1))
    skip = jnp.repeat(skip_gain, 64, axis=1)
    taps_bc = conv_bc_weight[0]
    taps = conv_x_weight[0]
    *decays, grow, weight, last = pl.pallas_call(
        pre_kernel,
        out_shape=(
            shape((T, CD), F32),
            shape((T, CD), F32),
            shape((KIDS, T, 3 * HD), BF16),
            shape((KIDS, T, 3 * HD), BF16),
            shape((KIDS, HD, N), F32),
        ),
        in_specs=[SMEM] + [VMEM] * 3,
        out_specs=tuple([VMEM] * 5),
        compiler_params=params(10),
        cost_estimate=cost(200_000_000, 5_000_000, 1_000_000),
        name="pre",
    )(lengths, inc, a_log, dt_bias)

    totals = pl.pallas_call(
        totals_kernel,
        out_shape=shape((KIDS, T), F32),
        in_specs=[VMEM] * 4,
        out_specs=VMEM,
        compiler_params=params(4),
        name="totals",
    )(part, r1, r2, r3)

    early = ()
    kept = {}
    for c in (1 - LATE, LATE):
        out_dims = ((KIDS, T, CD), (KIDS, T)) if c == LATE else ((T, CD), (1, T))
        result = pl.pallas_call(
            functools.partial(mid_kernel, c),
            out_shape=(
                shape(out_dims[0], BF16),
                shape(out_dims[1], F32),
                shape((T, CD), BF16),
                shape((T, CD), BF16),
                shape((T, 256), BF16),
            ),
            in_specs=[SMEM] * 2 + [VMEM] * (11 + len(early)),
            out_specs=tuple([VMEM] * 5),
            scratch_shapes=[
                pltpu.VMEM((72, 512), F32),
                pltpu.VMEM((8, CD), F32),
                pltpu.VMEM((T, CD), F32),
            ],
            compiler_params=params(12),
            cost_estimate=cost(100_000_000, 3_000_000, 500_000),
            name="mid%d" % c,
        )(
            section,
            lengths,
            messages[c],
            bc,
            taps_bc,
            streams_in,
            totals,
            input_norm_gain,
            taps,
            skip,
            out_gain,
            decays[c],
            grow,
            *early,
        )
        early = result[:2]
        kept[c] = result[2:]
    mid, mid_part = early
    mixes, reads, b_mats = zip(kept[0], kept[1])

    moved = lax.ppermute(mid, "section", [(0, 1), (1, 0)])
    q1, q2, q3 = [
        lax.ppermute(
            mid_part,
            ("section", "tensor"),
            [(c * tens + i, (1 - c) * tens + (i + k) % tens) for c in range(2) for i in range(tens)],
        )
        for k in range(1, tens)
    ]

    others = pl.pallas_call(
        others_kernel,
        out_shape=shape((KIDS, T), F32),
        in_specs=[VMEM] * 3,
        out_specs=VMEM,
        compiler_params=params(4),
        cost_estimate=cost(10_000_000_000, 100_000_000, 0),
        name="others",
    )(q1, q2, q3)

    out, new, x_out, bc_out = pl.pallas_call(
        last_kernel,
        out_shape=(
            shape((KIDS, T, CD), BF16),
            shape((KIDS, CD, N), BF16),
            shape((3, KIDS, CD), BF16),
            shape((KIDS, 3, 2, W), BF16),
        ),
        in_specs=[SMEM] + [VMEM] * 17,
        out_specs=(HBM, HBM, HBM, HBM),
        scratch_shapes=[
            pltpu.VMEM((KIDS, 72, CD), F32),
            pltpu.VMEM((KIDS, T, CD), F32),
            pltpu.VMEM((KIDS, T, CD), BF16),
            pltpu.VMEM((KIDS, 72, 512), F32),
            pltpu.VMEM((KIDS, T, CD), BF16),
            pltpu.VMEM((KIDS, CD, N), BF16),
            pltpu.VMEM((3, KIDS, CD), BF16),
            pltpu.VMEM((KIDS, 3, 2, W), BF16),
            pltpu.SemaphoreType.DMA((6,)),
            pltpu.SemaphoreType.DMA((KIDS, 2)),
        ],
        compiler_params=params(14),
        cost_estimate=cost(200_000_000, 5_000_000, 1_000_000),
        name="last",
    )(
        lengths,
        others,
        input_norm_gain,
        taps,
        skip,
        out_gain,
        bc,
        *b_mats,
        last,
        moved,
        weight,
        *mixes,
        *reads,
        *messages,
    )
    return (
        out[None],
        new.reshape(1, KIDS, HD, 64, N),
        jnp.transpose(x_out, (1, 0, 2))[None],
        bc_out[None],
    )


def solution(mesh):
    placed = (
        P("beam", None, "tensor"),
        P("section", "beam", "tensor", None, None),
        P("section", "beam", None, "tensor"),
        P("section", "beam", None, None, "tensor"),
        P("section", "beam", None, None, "tensor"),
        P("section", "beam", None, "tensor"),
        P(),
        P("beam"),
        P("section", "tensor"),
        P("section", None, "tensor"),
        P("section", None, None, "tensor"),
        P("section", "tensor"),
        P("section", "tensor"),
        P("section", "tensor"),
        P("section", "tensor"),
    )
    return jax.shard_map(
        on_device,
        mesh=mesh,
        in_specs=placed,
        out_specs=(
            P("section", "beam", None, "tensor"),
            P("section", "beam", "tensor", None, None),
            P("section", "beam", None, "tensor"),
            P("section", "beam", None, None, "tensor"),
        ),
        check_vma=False,
    )
```

```python
import functools

import jax
import jax.numpy as jnp
from jax import lax
from jax.experimental import pallas as pl
from jax.experimental.pallas import tpu as pltpu
from jax.sharding import PartitionSpec as P

CH = 8192
EPS = 1e-05
KIDS = 2
T = 64
CD = 2048
HD = 32
N = 128
W = 256
GC = 1024
F32 = jnp.float32
BF16 = jnp.bfloat16
HIGHEST = lax.Precision.HIGHEST
VMEM = pl.BlockSpec(memory_space=pltpu.VMEM)
SMEM = pl.BlockSpec(memory_space=pltpu.SMEM)
HBM = pl.BlockSpec(memory_space=pl.ANY)
BIG = 60
PARTS = 4
LATE = 1


def iota(shape, dim):
    return lax.broadcasted_iota(jnp.int32, shape, dim)


def as_row(col):
    size = col.shape[0]
    keep = iota((size, size), 0) == iota((size, size), 1)
    return jnp.sum(jnp.where(keep, col, 0.0), axis=0, keepdims=True)


def as_col(row):
    size = row.shape[1]
    keep = iota((size, size), 0) == iota((size, size), 1)
    return jnp.sum(jnp.where(keep, row, 0.0), axis=1, keepdims=True)


def silu(v):
    return 0.5 * v * (1.0 + jnp.tanh(0.5 * v))


def dot(a, b, dims, precision=None):
    return lax.dot_general(
        a, b, (dims, ((), ())), precision=precision, preferred_element_type=F32
    )


def three_parts(v):
    high = v.astype(BF16)
    rest = v - high.astype(F32)
    mid = rest.astype(BF16)
    low = (rest - mid.astype(F32)).astype(BF16)
    return [high, mid, low]


def pick_kernel(
    parents_in_ref,
    conv_x_in_ref,
    conv_bc_in_ref,
    state_in_ref,
    one_ref,
    two_ref,
    parents_ref,
    conv_x_ref,
    conv_bc_ref,
    state_ref,
    rows_ref,
    sems,
    out_sems,
):
    get_parents = pltpu.make_async_copy(parents_in_ref, parents_ref, sems.at[0])
    parts = [pl.ds(CD // PARTS * j, CD // PARTS) for j in range(PARTS)]
    get_states = [
        pltpu.make_async_copy(state_in_ref.at[i, at], state_ref.at[i, at], sems.at[3 + KIDS * j + i])
        for j, at in enumerate(parts)
        for i in range(KIDS)
    ]
    get_x = pltpu.make_async_copy(conv_x_in_ref, conv_x_ref, sems.at[1])
    get_bc = pltpu.make_async_copy(conv_bc_in_ref, conv_bc_ref, sems.at[2])
    for copy in (get_parents, get_x, get_bc, *get_states):
        copy.start()
    peers = lax.axis_size("beam")
    me = lax.axis_index("beam")
    get_parents.wait()
    picks = (
        lax.rem(parents_ref[KIDS * lax.rem(me + 1, peers)], KIDS),
        lax.rem(parents_ref[KIDS * lax.rem(me + peers - 1, peers) + 1], KIDS),
    )
    outs = (one_ref, two_ref)
    get_x.wait()
    get_bc.wait()
    puts = []
    for i in range(2):
        low = picks[i] == 0
        pieces = []
        for k in range(3):
            both = conv_x_ref[k].astype(F32)
            row = jnp.where(low, both[0:1], both[1:2])
            pieces += [row[:, N * j : N * (j + 1)] for j in range(CD // N)]
        for k in range(3):
            both = conv_bc_ref[picks[i], k].astype(F32)
            pieces += [both[p : p + 1, N * j : N * (j + 1)] for p in range(2) for j in range(2)]
        pieces.append(jnp.zeros((4, N), F32))
        rows_ref[i] = jnp.concatenate(pieces, axis=0).astype(BF16)
        puts.append(pltpu.make_async_copy(rows_ref.at[i], outs[i].at[CD:], out_sems.at[i, PARTS]))
        puts[-1].start()
    for j, at in enumerate(parts):
        for i in range(KIDS):
            get_states[KIDS * j + i].wait()
        for i in range(2):
            puts.append(
                pltpu.make_async_copy(
                    state_ref.at[picks[i], at], outs[i].at[at], out_sems.at[i, j]
                )
            )
            puts[-1].start()
    for copy in puts:
        copy.wait()


def square_kernel(stream_ref, part_ref):
    for c in range(KIDS):
        s = stream_ref[c].astype(F32)
        part_ref[c : c + 1, :] = as_row(jnp.sum(s * s, axis=1, keepdims=True))


def lay_rows(rows, past_ref):
    for k in range(3):
        for j in range(CD // N):
            at = 16 * k + j
            past_ref[5 + k : 6 + k, N * j : N * (j + 1)] = rows[at : at + 1, :]


def delayed(value, past, steps):
    rolled = pltpu.roll(value, steps, 0)
    head = jnp.where(iota(past.shape, 0) < steps, pltpu.roll(past, steps, 0), rolled[:8])
    return jnp.concatenate([head, rolled[8:]], axis=0)


def scaled_x(s, at, scale, gain_ref):
    return (s * scale * gain_ref[:, at]).astype(BF16).astype(F32)


def fresh_x(x_in, at, taps_ref, valid, past_ref):
    acc = taps_ref[3:4, at] * x_in
    for k in range(1, 4):
        acc = acc + taps_ref[3 - k : 4 - k, at] * delayed(x_in, past_ref[:8, at], k)
    return silu(acc) * valid


def head_masks():
    lane = iota((T, W), 1) // 64
    return [jnp.where(lane == j, 1.0, 0.0).astype(BF16) for j in range(4)]


def intra(mix, x, masks):
    xb = x.astype(BF16)
    return dot(mix, jnp.concatenate([xb * mask for mask in masks], axis=0), ((1,), (0,)))


def head_onehot():
    row = iota((N, W), 0)
    same = row % HD == iota((N, W), 1) // 64
    return jnp.where(same & (row < 3 * HD), 1.0, 0.0).astype(BF16)


def spread(parts, onehot, q):
    turned = pltpu.roll(parts, (N - 4 * q) % N, 1).astype(BF16) if q else parts.astype(BF16)
    return dot(turned, onehot, ((1,), (0,)))


def halves(v):
    return v[:, :N] + v[:, N:]


def fresh_bc(rows, bc, taps_ref, pbc_ref):
    for k in range(3):
        for j in range(4):
            at = 48 + 4 * k + j
            pbc_ref[5 + k : 6 + k, N * j : N * (j + 1)] = rows[at : at + 1, :]
    pbc_ref[8:72, :] = bc.astype(F32)
    acc = 0.0
    for k in range(4):
        taps = jnp.concatenate([taps_ref[k, 0:1, :], taps_ref[k, 1:2, :]], axis=1)
        acc = acc + taps * pbc_ref[5 + k : 69 + k, :]
    return silu(acc)


def valid_col(length):
    return jnp.where(iota((T, 1), 0) < length, 1.0, 0.0)


def spread_heads(compact):
    onehot = jnp.where(iota((HD, CD), 0) == iota((HD, CD), 1) // 64, 1.0, 0.0).astype(BF16)
    onehot = jnp.concatenate([onehot] * 3, axis=0)
    return dot(jnp.concatenate(three_parts(compact), axis=0), onehot, ((0,), (0,)))


def pre_kernel(
    len_ref, inc_ref, log_ref, bias_ref, decay0_ref, decay1_ref, grow_ref, weight_ref, last_ref
):
    rate = as_col(jnp.exp(log_ref[...]))
    bias = as_col(bias_ref[...])
    upper = jnp.where(iota((T, T), 0) <= iota((T, T), 1), 1.0, 0.0)
    diag = iota((T, CD), 1) % T == iota((T, CD), 0)
    causal = iota((T, CD), 0) >= iota((T, CD), 1) % T
    for c in range(KIDS):
        valid_row = jnp.where(iota((1, T), 1) < len_ref[c], 1.0, 0.0)
        raw = inc_ref[c] + bias
        dt = (jnp.maximum(raw, 0.0) + jnp.log1p(jnp.exp(-jnp.abs(raw)))) * valid_row
        cum = dot(-dt * rate, upper, ((1,), (0,)), HIGHEST)
        final = cum[:, T - 1 : T]
        last_ref[c] = jnp.broadcast_to(jnp.exp(final), (HD, N))
        for ref, value in ((grow_ref, jnp.exp(cum)), (weight_ref, jnp.exp(final - cum) * dt)):
            parts = [part.astype(F32) for part in three_parts(value)]
            ref[c] = jnp.concatenate([*parts, jnp.zeros_like(value)], axis=0).T
        edt = spread_heads(dt)
        ecum = spread_heads(cum)
        row_dt = jnp.sum(jnp.where(diag, edt, 0.0), axis=0, keepdims=True)
        row_cum = jnp.sum(jnp.where(diag, ecum, 0.0), axis=0, keepdims=True)
        gap = jnp.exp(jnp.minimum(ecum - row_cum, 0.0))
        (decay0_ref, decay1_ref)[c][...] = jnp.where(causal, gap * row_dt, 0.0)


def mid_kernel(
    c,
    sec_ref,
    len_ref,
    message_ref,
    bc_ref,
    taps_bc_ref,
    stream_ref,
    totals_ref,
    gain_in_ref,
    taps_ref,
    skip_ref,
    gain_ref,
    decay_ref,
    grow_ref,
    *refs,
):
    if c == LATE:
        early_ref, early_part_ref = refs[:2]
        refs = refs[2:]
    out_ref, part_ref, mix_ref, read_ref, b_ref, pbc_ref, past_ref, y_ref = refs
    rows = message_ref[CD:, :].astype(F32)
    bc = fresh_bc(rows, bc_ref[c], taps_bc_ref, pbc_ref)
    b_ref[...] = bc[:, :W].astype(BF16)
    inner = []
    for g in range(2):
        bg = bc[:, N * g : N * (g + 1)]
        cg = bc[:, W + N * g : W + N * (g + 1)]
        ch, cl = three_parts(cg)[:2]
        bh, bl = three_parts(bg)[:2]
        both = jnp.concatenate([bh, bl, bh], axis=1)
        both = jnp.concatenate([both] * 4, axis=0)
        inner.append(dot(jnp.concatenate([ch, ch, cl], axis=1), both, ((1,), (1,))))
    cb = bc[:, W:].astype(BF16)
    valid = valid_col(len_ref[c])
    scale = lax.rsqrt(as_col(totals_ref[c : c + 1]) / CH + EPS)
    lay_rows(rows, past_ref)
    masks = head_masks()
    onehot = head_onehot()
    sums = [0.0, 0.0]
    for q in range(CD // W):
        at = slice(W * q, W * (q + 1))
        g = q // 4
        s = stream_ref[c, :, at].astype(F32)
        x = fresh_x(scaled_x(s, at, scale, gain_in_ref), at, taps_ref, valid, past_ref)
        mix = (decay_ref[:, at] * inner[g]).astype(BF16)
        mix_ref[:, at] = mix
        read = dot(cb[:, N * g : N * (g + 1)], message_ref[at, :], ((1,), (1,)))
        read = read * spread(grow_ref[c], onehot, q)
        read_ref[:, at] = read.astype(BF16)
        y = intra(mix, x, masks) + skip_ref[:, at] * x + read
        y_ref[:, at] = y
        sums[g] = sums[g] + halves(y * y)
    norm = [
        lax.rsqrt(jnp.sum(v, axis=1, keepdims=True) * (1.0 / GC) + EPS) * valid for v in sums
    ]
    squares = 0.0
    first = sec_ref[0] == 0
    for q in range(CD // W):
        at = slice(W * q, W * (q + 1))
        z = y_ref[:, at] * norm[q // 4] * gain_ref[:, at]
        out = (stream_ref[c, :, at].astype(F32) + jnp.where(first, z, 0.0)).astype(BF16)
        s = out.astype(F32)
        squares = squares + halves(s * s)
        if c == LATE:
            out_ref[c, :, at] = out
            out_ref[1 - c, :, at] = early_ref[:, at]
        else:
            out_ref[:, at] = out
    part = as_row(jnp.sum(squares, axis=1, keepdims=True))
    if c == LATE:
        part_ref[c : c + 1, :] = part
        part_ref[1 - c : 2 - c, :] = early_part_ref[...]
    else:
        part_ref[...] = part


def totals_kernel(p_ref, r1_ref, r2_ref, r3_ref, totals_ref):
    totals_ref[...] = p_ref[...] + r1_ref[...] + r2_ref[...] + r3_ref[...]


def others_kernel(q1_ref, q2_ref, q3_ref, others_ref):
    others_ref[...] = q1_ref[...] + q2_ref[...] + q3_ref[...]


def last_kernel(
    len_ref,
    others_ref,
    gain_in_ref,
    taps_ref,
    skip_ref,
    gain_ref,
    bc_ref,
    b0_ref,
    b1_ref,
    last_ref,
    moved_ref,
    weight_ref,
    mix0_ref,
    mix1_ref,
    read0_ref,
    read1_ref,
    message0_ref,
    message1_ref,
    out_to_ref,
    new_to_ref,
    x_to_ref,
    bc_to_ref,
    px_ref,
    y_ref,
    xw_ref,
    pbc_ref,
    out_ref,
    new_ref,
    x_out_ref,
    bc_out_ref,
    sems,
    new_sems,
):
    puts = []

    def send(source, target, sem):
        puts.append(pltpu.make_async_copy(source, target, sem))
        puts[-1].start()

    masks = head_masks()
    onehot = head_onehot()
    chunks = [slice(W * q, W * (q + 1)) for q in range(CD // W)]
    messages = (message0_ref, message1_ref)
    valids = [valid_col(len_ref[c]) for c in range(KIDS)]
    scales = []
    for c in range(KIDS):
        squares = 0.0
        for at in chunks:
            s = moved_ref[c, :, at].astype(F32)
            squares = squares + halves(s * s)
        total = jnp.sum(squares, axis=1, keepdims=True) + as_col(others_ref[c : c + 1])
        scales.append(lax.rsqrt(total / CH + EPS))
        rows = messages[c][CD:, :].astype(F32)
        lay_rows(rows, px_ref.at[c])
        for k in range(3):
            for j in range(4):
                at = 48 + 4 * k + j
                pbc_ref[c, 5 + k : 6 + k, N * j : N * (j + 1)] = rows[at : at + 1, :]
        pbc_ref[c, 8:72, :] = bc_ref[c].astype(F32)
    sums = [[0.0, 0.0] for _ in range(KIDS)]
    for q, at in enumerate(chunks):
        for c in range(KIDS):
            x_in = scaled_x(moved_ref[c, :, at].astype(F32), at, scales[c], gain_in_ref)
            px_ref[c, 8:72, at] = x_in
            x = fresh_x(x_in, at, taps_ref, valids[c], px_ref.at[c])
            xw_ref[c, :, at] = (x * spread(weight_ref[c], onehot, q)).astype(BF16)
            y = intra((mix0_ref, mix1_ref)[c][:, at], x, masks) + skip_ref[:, at] * x
            y = y + (read0_ref, read1_ref)[c][:, at].astype(F32)
            y_ref[c, :, at] = y
            sums[c][q // 4] = sums[c][q // 4] + halves(y * y)
    for c in range(KIDS):
        norm = [
            lax.rsqrt(jnp.sum(v, axis=1, keepdims=True) * (1.0 / GC) + EPS) * valids[c]
            for v in sums[c]
        ]
        for q, at in enumerate(chunks):
            z = y_ref[c, :, at] * norm[q // 4] * gain_ref[:, at]
            out_ref[c, :, at] = (moved_ref[c, :, at].astype(F32) + z).astype(BF16)
    for c in range(KIDS):
        send(out_ref.at[c], out_to_ref.at[c], sems.at[4 + c])
    for k in range(3):
        tails = [px_ref[c, pl.ds(5 + len_ref[c] + k, 1), :] for c in range(KIDS)]
        x_out_ref[k] = jnp.concatenate(tails, axis=0).astype(BF16)
        for c in range(KIDS):
            row = pbc_ref[c, pl.ds(5 + len_ref[c] + k, 1), :]
            bc_out_ref[c, k] = jnp.concatenate([row[:, :W], row[:, W:]], axis=0).astype(BF16)
    send(x_out_ref, x_to_ref, sems.at[2])
    send(bc_out_ref, bc_to_ref, sems.at[3])
    for g in range(2):
        for c in range(KIDS):
            for q in range(4 * g, 4 * g + 4):
                b = (b0_ref, b1_ref)[c][:, N * g : N * (g + 1)]
                fresh = dot(xw_ref[c, :, chunks[q]], b, ((0,), (0,)))
                for j in range(4):
                    rows_at = slice(W * q + 64 * j, W * q + 64 * (j + 1))
                    h = 4 * q + j
                    new_ref[c, rows_at, :] = (
                        last_ref[c, h : h + 1, :] * messages[c][rows_at, :].astype(F32)
                        + fresh[64 * j : 64 * (j + 1)]
                    ).astype(BF16)
            half = pl.ds(GC * g, GC)
            send(new_ref.at[c, half], new_to_ref.at[c, half], new_sems.at[c, g])
    for copy in puts:
        copy.wait()


def shape(dims, kind):
    return jax.ShapeDtypeStruct(dims, kind)


def params(mib):
    return pltpu.CompilerParams(vmem_limit_bytes=mib * 2**20)


def cost(flops, moved, exps=0):
    return pl.CostEstimate(flops=flops, bytes_accessed=moved, transcendentals=exps)


def on_device(
    streams_in,
    beam_state_cache,
    conv_x_cache,
    conv_bc_cache,
    bc_inputs,
    unbiased_increments,
    parents,
    lengths,
    input_norm_gain,
    conv_x_weight,
    conv_bc_weight,
    a_log,
    dt_bias,
    skip_gain,
    out_gain,
):
    tens = lax.axis_size("tensor")
    peers = lax.axis_size("beam")
    section = lax.axis_index("section").astype(jnp.int32)[None]
    message = shape((CD + 64, N), BF16)
    fwd, bwd = pl.pallas_call(
        pick_kernel,
        out_shape=(message, message),
        in_specs=[HBM] * 4,
        out_specs=(HBM, HBM),
        scratch_shapes=[
            pltpu.SMEM(parents.shape, jnp.int32),
            pltpu.VMEM((3, KIDS, CD), BF16),
            pltpu.VMEM((KIDS, 3, 2, 256), BF16),
            pltpu.VMEM((KIDS, CD, N), BF16),
            pltpu.VMEM((2, 64, N), BF16),
            pltpu.SemaphoreType.DMA((3 + KIDS * PARTS,)),
            pltpu.SemaphoreType.DMA((2, PARTS + 1)),
        ],
        compiler_params=params(BIG),
        name="pick",
    )(
        parents,
        jnp.transpose(conv_x_cache[0], (1, 0, 2)),
        conv_bc_cache[0],
        beam_state_cache[0].reshape(KIDS, CD, N),
    )
    part = pl.pallas_call(
        square_kernel,
        out_shape=shape((KIDS, T), F32),
        in_specs=[VMEM],
        out_specs=VMEM,
        compiler_params=params(4),
        name="square",
    )(streams_in)

    def along(value, axis, steps):
        size = lax.axis_size(axis)
        return lax.ppermute(value, axis, [(i, (i + steps) % size) for i in range(size)])

    messages = (along(fwd, "beam", 1), along(bwd, "beam", -1))
    r1, r2, r3 = [along(part, "tensor", k) for k in range(1, tens)]

    bc = bc_inputs[0].reshape(KIDS, T, 512)
    inc = jnp.transpose(unbiased_increments[0], (0, 2, 1))
    skip = jnp.repeat(skip_gain, 64, axis=1)
    taps_bc = conv_bc_weight[0]
    taps = conv_x_weight[0]
    *decays, grow, weight, last = pl.pallas_call(
        pre_kernel,
        out_shape=(
            shape((T, CD), F32),
            shape((T, CD), F32),
            shape((KIDS, T, N), F32),
            shape((KIDS, T, N), F32),
            shape((KIDS, HD, N), F32),
        ),
        in_specs=[SMEM] + [VMEM] * 3,
        out_specs=tuple([VMEM] * 5),
        compiler_params=params(10),
        cost_estimate=cost(200_000_000, 5_000_000, 1_000_000),
        name="pre",
    )(lengths, inc, a_log, dt_bias)

    totals = pl.pallas_call(
        totals_kernel,
        out_shape=shape((KIDS, T), F32),
        in_specs=[VMEM] * 4,
        out_specs=VMEM,
        compiler_params=params(4),
        name="totals",
    )(part, r1, r2, r3)

    early = ()
    kept = {}
    for c in (1 - LATE, LATE):
        out_dims = ((KIDS, T, CD), (KIDS, T)) if c == LATE else ((T, CD), (1, T))
        result = pl.pallas_call(
            functools.partial(mid_kernel, c),
            out_shape=(
                shape(out_dims[0], BF16),
                shape(out_dims[1], F32),
                shape((T, CD), BF16),
                shape((T, CD), BF16),
                shape((T, 256), BF16),
            ),
            in_specs=[SMEM] * 2 + [VMEM] * (11 + len(early)),
            out_specs=tuple([VMEM] * 5),
            scratch_shapes=[
                pltpu.VMEM((72, 512), F32),
                pltpu.VMEM((8, CD), F32),
                pltpu.VMEM((T, CD), F32),
            ],
            compiler_params=params(12),
            cost_estimate=cost(100_000_000, 3_000_000, 500_000),
            name="mid%d" % c,
        )(
            section,
            lengths,
            messages[c],
            bc,
            taps_bc,
            streams_in,
            totals,
            input_norm_gain,
            taps,
            skip,
            out_gain,
            decays[c],
            grow,
            *early,
        )
        early = result[:2]
        kept[c] = result[2:]
    mid, mid_part = early
    mixes, reads, b_mats = zip(kept[0], kept[1])

    moved = lax.ppermute(mid, "section", [(0, 1), (1, 0)])
    q1, q2, q3 = [
        lax.ppermute(
            mid_part,
            ("section", "tensor"),
            [(c * tens + i, (1 - c) * tens + (i + k) % tens) for c in range(2) for i in range(tens)],
        )
        for k in range(1, tens)
    ]

    others = pl.pallas_call(
        others_kernel,
        out_shape=shape((KIDS, T), F32),
        in_specs=[VMEM] * 3,
        out_specs=VMEM,
        compiler_params=params(4),
        cost_estimate=cost(10_000_000_000, 100_000_000, 0),
        name="others",
    )(q1, q2, q3)

    out, new, x_out, bc_out = pl.pallas_call(
        last_kernel,
        out_shape=(
            shape((KIDS, T, CD), BF16),
            shape((KIDS, CD, N), BF16),
            shape((3, KIDS, CD), BF16),
            shape((KIDS, 3, 2, W), BF16),
        ),
        in_specs=[SMEM] + [VMEM] * 17,
        out_specs=(HBM, HBM, HBM, HBM),
        scratch_shapes=[
            pltpu.VMEM((KIDS, 72, CD), F32),
            pltpu.VMEM((KIDS, T, CD), F32),
            pltpu.VMEM((KIDS, T, CD), BF16),
            pltpu.VMEM((KIDS, 72, 512), F32),
            pltpu.VMEM((KIDS, T, CD), BF16),
            pltpu.VMEM((KIDS, CD, N), BF16),
            pltpu.VMEM((3, KIDS, CD), BF16),
            pltpu.VMEM((KIDS, 3, 2, W), BF16),
            pltpu.SemaphoreType.DMA((6,)),
            pltpu.SemaphoreType.DMA((KIDS, 2)),
        ],
        compiler_params=params(14),
        cost_estimate=cost(200_000_000, 5_000_000, 1_000_000),
        name="last",
    )(
        lengths,
        others,
        input_norm_gain,
        taps,
        skip,
        out_gain,
        bc,
        *b_mats,
        last,
        moved,
        weight,
        *mixes,
        *reads,
        *messages,
    )
    return (
        out[None],
        new.reshape(1, KIDS, HD, 64, N),
        jnp.transpose(x_out, (1, 0, 2))[None],
        bc_out[None],
    )


def solution(mesh):
    placed = (
        P("beam", None, "tensor"),
        P("section", "beam", "tensor", None, None),
        P("section", "beam", None, "tensor"),
        P("section", "beam", None, None, "tensor"),
        P("section", "beam", None, None, "tensor"),
        P("section", "beam", None, "tensor"),
        P(),
        P("beam"),
        P("section", "tensor"),
        P("section", None, "tensor"),
        P("section", None, None, "tensor"),
        P("section", "tensor"),
        P("section", "tensor"),
        P("section", "tensor"),
        P("section", "tensor"),
    )
    return jax.shard_map(
        on_device,
        mesh=mesh,
        in_specs=placed,
        out_specs=(
            P("section", "beam", None, "tensor"),
            P("section", "beam", "tensor", None, None),
            P("section", "beam", None, "tensor"),
            P("section", "beam", None, None, "tensor"),
        ),
        check_vma=False,
    )
```

```python
import functools

import jax
import jax.numpy as jnp
from jax import lax
from jax.experimental import pallas as pl
from jax.experimental.pallas import tpu as pltpu
from jax.sharding import PartitionSpec as P

CH = 8192
EPS = 1e-05
KIDS = 2
T = 64
CD = 2048
HD = 32
N = 128
W = 256
GC = 1024
F32 = jnp.float32
BF16 = jnp.bfloat16
HIGHEST = lax.Precision.HIGHEST
VMEM = pl.BlockSpec(memory_space=pltpu.VMEM)
SMEM = pl.BlockSpec(memory_space=pltpu.SMEM)
HBM = pl.BlockSpec(memory_space=pl.ANY)
BIG = 60
PARTS = 4
LATE = 0
EXTRA = 16


def iota(shape, dim):
    return lax.broadcasted_iota(jnp.int32, shape, dim)


def as_row(col):
    size = col.shape[0]
    keep = iota((size, size), 0) == iota((size, size), 1)
    return jnp.sum(jnp.where(keep, col, 0.0), axis=0, keepdims=True)


def as_col(row):
    size = row.shape[1]
    keep = iota((size, size), 0) == iota((size, size), 1)
    return jnp.sum(jnp.where(keep, row, 0.0), axis=1, keepdims=True)


def silu(v):
    return 0.5 * v * (1.0 + jnp.tanh(0.5 * v))


def dot(a, b, dims, precision=None):
    return lax.dot_general(
        a, b, (dims, ((), ())), precision=precision, preferred_element_type=F32
    )


def three_parts(v):
    high = v.astype(BF16)
    rest = v - high.astype(F32)
    mid = rest.astype(BF16)
    low = (rest - mid.astype(F32)).astype(BF16)
    return [high, mid, low]


def pick_kernel(
    parents_in_ref,
    conv_x_in_ref,
    conv_bc_in_ref,
    state_in_ref,
    one_ref,
    two_ref,
    parents_ref,
    conv_x_ref,
    conv_bc_ref,
    state_ref,
    rows_ref,
    sems,
    out_sems,
):
    get_parents = pltpu.make_async_copy(parents_in_ref, parents_ref, sems.at[0])
    parts = [pl.ds(CD // PARTS * j, CD // PARTS) for j in range(PARTS)]
    get_states = [
        pltpu.make_async_copy(state_in_ref.at[i, at], state_ref.at[i, at], sems.at[3 + KIDS * j + i])
        for j, at in enumerate(parts)
        for i in range(KIDS)
    ]
    get_x = pltpu.make_async_copy(conv_x_in_ref, conv_x_ref, sems.at[1])
    get_bc = pltpu.make_async_copy(conv_bc_in_ref, conv_bc_ref, sems.at[2])
    for copy in (get_parents, get_x, get_bc, *get_states):
        copy.start()
    peers = lax.axis_size("beam")
    me = lax.axis_index("beam")
    get_parents.wait()
    picks = (
        lax.rem(parents_ref[KIDS * lax.rem(me + 1, peers)], KIDS),
        lax.rem(parents_ref[KIDS * lax.rem(me + peers - 1, peers) + 1], KIDS),
    )
    outs = (one_ref, two_ref)
    get_x.wait()
    get_bc.wait()
    puts = []
    for i in range(2):
        low = picks[i] == 0
        pieces = []
        for k in range(3):
            both = conv_x_ref[k].astype(F32)
            row = jnp.where(low, both[0:1], both[1:2])
            pieces += [row[:, N * j : N * (j + 1)] for j in range(CD // N)]
        for k in range(3):
            both = conv_bc_ref[picks[i], k].astype(F32)
            pieces += [both[p : p + 1, N * j : N * (j + 1)] for p in range(2) for j in range(2)]
        pieces.append(jnp.zeros((4, N), F32))
        rows_ref[i] = jnp.concatenate(pieces, axis=0).astype(BF16)
        puts.append(pltpu.make_async_copy(rows_ref.at[i], outs[i].at[pl.ds(CD, 64)], out_sems.at[i, PARTS]))
        puts[-1].start()
    for j, at in enumerate(parts):
        for i in range(KIDS):
            get_states[KIDS * j + i].wait()
        for i in range(2):
            puts.append(
                pltpu.make_async_copy(
                    state_ref.at[picks[i], at], outs[i].at[at], out_sems.at[i, j]
                )
            )
            puts[-1].start()
    puts.append(
        pltpu.make_async_copy(
            rows_ref.at[0, :EXTRA], one_ref.at[pl.ds(CD + 64, EXTRA)], out_sems.at[2, 0]
        )
    )
    puts[-1].start()
    for copy in puts:
        copy.wait()


def square_kernel(stream_ref, part_ref):
    for c in range(KIDS):
        s = stream_ref[c].astype(F32)
        part_ref[c : c + 1, :] = as_row(jnp.sum(s * s, axis=1, keepdims=True))


def lay_rows(rows, past_ref):
    for k in range(3):
        for j in range(CD // N):
            at = 16 * k + j
            past_ref[5 + k : 6 + k, N * j : N * (j + 1)] = rows[at : at + 1, :]


def delayed(value, past, steps):
    rolled = pltpu.roll(value, steps, 0)
    head = jnp.where(iota(past.shape, 0) < steps, pltpu.roll(past, steps, 0), rolled[:8])
    return jnp.concatenate([head, rolled[8:]], axis=0)


def scaled_x(s, at, scale, gain_ref):
    return (s * scale * gain_ref[:, at]).astype(BF16).astype(F32)


def fresh_x(x_in, at, taps_ref, valid, past_ref):
    acc = taps_ref[3:4, at] * x_in
    for k in range(1, 4):
        acc = acc + taps_ref[3 - k : 4 - k, at] * delayed(x_in, past_ref[:8, at], k)
    return silu(acc) * valid


def head_masks():
    lane = iota((T, W), 1) // 64
    return [jnp.where(lane == j, 1.0, 0.0).astype(BF16) for j in range(4)]


def intra(mix, x, masks):
    xb = x.astype(BF16)
    return dot(mix, jnp.concatenate([xb * mask for mask in masks], axis=0), ((1,), (0,)))


def head_onehot():
    row = iota((N, W), 0)
    same = row % HD == iota((N, W), 1) // 64
    return jnp.where(same & (row < 3 * HD), 1.0, 0.0).astype(BF16)


def spread(parts, onehot, q):
    turned = pltpu.roll(parts, (N - 4 * q) % N, 1).astype(BF16) if q else parts.astype(BF16)
    return dot(turned, onehot, ((1,), (0,)))


def halves(v):
    return v[:, :N] + v[:, N:]


def fresh_bc(rows, bc, taps_ref, pbc_ref):
    for k in range(3):
        for j in range(4):
            at = 48 + 4 * k + j
            pbc_ref[5 + k : 6 + k, N * j : N * (j + 1)] = rows[at : at + 1, :]
    pbc_ref[8:72, :] = bc.astype(F32)
    acc = 0.0
    for k in range(4):
        taps = jnp.concatenate([taps_ref[k, 0:1, :], taps_ref[k, 1:2, :]], axis=1)
        acc = acc + taps * pbc_ref[5 + k : 69 + k, :]
    return silu(acc)


def valid_col(length):
    return jnp.where(iota((T, 1), 0) < length, 1.0, 0.0)


def spread_heads(compact):
    onehot = jnp.where(iota((HD, CD), 0) == iota((HD, CD), 1) // 64, 1.0, 0.0).astype(BF16)
    onehot = jnp.concatenate([onehot] * 3, axis=0)
    return dot(jnp.concatenate(three_parts(compact), axis=0), onehot, ((0,), (0,)))


def pre_kernel(
    len_ref, inc_ref, log_ref, bias_ref, decay0_ref, decay1_ref, grow_ref, weight_ref, last_ref
):
    rate = as_col(jnp.exp(log_ref[...]))
    bias = as_col(bias_ref[...])
    upper = jnp.where(iota((T, T), 0) <= iota((T, T), 1), 1.0, 0.0)
    diag = iota((T, CD), 1) % T == iota((T, CD), 0)
    causal = iota((T, CD), 0) >= iota((T, CD), 1) % T
    for c in range(KIDS):
        valid_row = jnp.where(iota((1, T), 1) < len_ref[c], 1.0, 0.0)
        raw = inc_ref[c] + bias
        dt = (jnp.maximum(raw, 0.0) + jnp.log1p(jnp.exp(-jnp.abs(raw)))) * valid_row
        cum = dot(-dt * rate, upper, ((1,), (0,)), HIGHEST)
        final = cum[:, T - 1 : T]
        last_ref[c] = jnp.broadcast_to(jnp.exp(final), (HD, N))
        for ref, value in ((grow_ref, jnp.exp(cum)), (weight_ref, jnp.exp(final - cum) * dt)):
            parts = [part.astype(F32) for part in three_parts(value)]
            ref[c] = jnp.concatenate([*parts, jnp.zeros_like(value)], axis=0).T
        edt = spread_heads(dt)
        ecum = spread_heads(cum)
        row_dt = jnp.sum(jnp.where(diag, edt, 0.0), axis=0, keepdims=True)
        row_cum = jnp.sum(jnp.where(diag, ecum, 0.0), axis=0, keepdims=True)
        gap = jnp.exp(jnp.minimum(ecum - row_cum, 0.0))
        (decay0_ref, decay1_ref)[c][...] = jnp.where(causal, gap * row_dt, 0.0)


def mid_kernel(
    c,
    sec_ref,
    len_ref,
    message_ref,
    bc_ref,
    taps_bc_ref,
    stream_ref,
    totals_ref,
    gain_in_ref,
    taps_ref,
    skip_ref,
    gain_ref,
    decay_ref,
    grow_ref,
    *refs,
):
    if c == LATE:
        early_ref, early_part_ref = refs[:2]
        refs = refs[2:]
    out_ref, part_ref, mix_ref, read_ref, b_ref, pbc_ref, past_ref, y_ref = refs
    rows = message_ref[CD : CD + 64, :].astype(F32)
    bc = fresh_bc(rows, bc_ref[c], taps_bc_ref, pbc_ref)
    b_ref[...] = bc[:, :W].astype(BF16)
    inner = []
    for g in range(2):
        bg = bc[:, N * g : N * (g + 1)]
        cg = bc[:, W + N * g : W + N * (g + 1)]
        ch, cl = three_parts(cg)[:2]
        bh, bl = three_parts(bg)[:2]
        both = jnp.concatenate([bh, bl, bh], axis=1)
        both = jnp.concatenate([both] * 4, axis=0)
        inner.append(dot(jnp.concatenate([ch, ch, cl], axis=1), both, ((1,), (1,))))
    cb = bc[:, W:].astype(BF16)
    valid = valid_col(len_ref[c])
    scale = lax.rsqrt(as_col(totals_ref[c : c + 1]) / CH + EPS)
    lay_rows(rows, past_ref)
    masks = head_masks()
    onehot = head_onehot()
    sums = [0.0, 0.0]
    for q in range(CD // W):
        at = slice(W * q, W * (q + 1))
        g = q // 4
        s = stream_ref[c, :, at].astype(F32)
        x = fresh_x(scaled_x(s, at, scale, gain_in_ref), at, taps_ref, valid, past_ref)
        mix = (decay_ref[:, at] * inner[g]).astype(BF16)
        mix_ref[:, at] = mix
        read = dot(cb[:, N * g : N * (g + 1)], message_ref[at, :], ((1,), (1,)))
        read = read * spread(grow_ref[c], onehot, q)
        read_ref[:, at] = read.astype(BF16)
        y = intra(mix, x, masks) + skip_ref[:, at] * x + read
        y_ref[:, at] = y
        sums[g] = sums[g] + halves(y * y)
    norm = [
        lax.rsqrt(jnp.sum(v, axis=1, keepdims=True) * (1.0 / GC) + EPS) * valid for v in sums
    ]
    squares = 0.0
    first = sec_ref[0] == 0
    for q in range(CD // W):
        at = slice(W * q, W * (q + 1))
        z = y_ref[:, at] * norm[q // 4] * gain_ref[:, at]
        out = (stream_ref[c, :, at].astype(F32) + jnp.where(first, z, 0.0)).astype(BF16)
        s = out.astype(F32)
        squares = squares + halves(s * s)
        if c == LATE:
            out_ref[c, :, at] = out
            out_ref[1 - c, :, at] = early_ref[:, at]
        else:
            out_ref[:, at] = out
    part = as_row(jnp.sum(squares, axis=1, keepdims=True))
    if c == LATE:
        part_ref[c : c + 1, :] = part
        part_ref[1 - c : 2 - c, :] = early_part_ref[...]
    else:
        part_ref[...] = part


def totals_kernel(p_ref, r1_ref, r2_ref, r3_ref, totals_ref):
    totals_ref[...] = p_ref[...] + r1_ref[...] + r2_ref[...] + r3_ref[...]


def others_kernel(q1_ref, q2_ref, q3_ref, others_ref):
    others_ref[...] = q1_ref[...] + q2_ref[...] + q3_ref[...]


def last_kernel(
    len_ref,
    others_ref,
    gain_in_ref,
    taps_ref,
    skip_ref,
    gain_ref,
    bc_ref,
    b0_ref,
    b1_ref,
    last_ref,
    moved_ref,
    weight_ref,
    mix0_ref,
    mix1_ref,
    read0_ref,
    read1_ref,
    message0_ref,
    message1_ref,
    out_to_ref,
    new_to_ref,
    x_to_ref,
    bc_to_ref,
    px_ref,
    y_ref,
    xw_ref,
    pbc_ref,
    out_ref,
    new_ref,
    x_out_ref,
    bc_out_ref,
    sems,
    new_sems,
):
    puts = []

    def send(source, target, sem):
        puts.append(pltpu.make_async_copy(source, target, sem))
        puts[-1].start()

    masks = head_masks()
    onehot = head_onehot()
    chunks = [slice(W * q, W * (q + 1)) for q in range(CD // W)]
    messages = (message0_ref, message1_ref)
    valids = [valid_col(len_ref[c]) for c in range(KIDS)]
    scales = []
    for c in range(KIDS):
        squares = 0.0
        for at in chunks:
            s = moved_ref[c, :, at].astype(F32)
            squares = squares + halves(s * s)
        total = jnp.sum(squares, axis=1, keepdims=True) + as_col(others_ref[c : c + 1])
        scales.append(lax.rsqrt(total / CH + EPS))
        rows = messages[c][CD : CD + 64, :].astype(F32)
        lay_rows(rows, px_ref.at[c])
        for k in range(3):
            for j in range(4):
                at = 48 + 4 * k + j
                pbc_ref[c, 5 + k : 6 + k, N * j : N * (j + 1)] = rows[at : at + 1, :]
        pbc_ref[c, 8:72, :] = bc_ref[c].astype(F32)
    sums = [[0.0, 0.0] for _ in range(KIDS)]
    for q, at in enumerate(chunks):
        for c in range(KIDS):
            x_in = scaled_x(moved_ref[c, :, at].astype(F32), at, scales[c], gain_in_ref)
            px_ref[c, 8:72, at] = x_in
            x = fresh_x(x_in, at, taps_ref, valids[c], px_ref.at[c])
            xw_ref[c, :, at] = (x * spread(weight_ref[c], onehot, q)).astype(BF16)
            y = intra((mix0_ref, mix1_ref)[c][:, at], x, masks) + skip_ref[:, at] * x
            y = y + (read0_ref, read1_ref)[c][:, at].astype(F32)
            y_ref[c, :, at] = y
            sums[c][q // 4] = sums[c][q // 4] + halves(y * y)
    for c in range(KIDS):
        norm = [
            lax.rsqrt(jnp.sum(v, axis=1, keepdims=True) * (1.0 / GC) + EPS) * valids[c]
            for v in sums[c]
        ]
        for q, at in enumerate(chunks):
            z = y_ref[c, :, at] * norm[q // 4] * gain_ref[:, at]
            out_ref[c, :, at] = (moved_ref[c, :, at].astype(F32) + z).astype(BF16)
    for c in range(KIDS):
        send(out_ref.at[c], out_to_ref.at[c], sems.at[4 + c])
    for k in range(3):
        tails = [px_ref[c, pl.ds(5 + len_ref[c] + k, 1), :] for c in range(KIDS)]
        x_out_ref[k] = jnp.concatenate(tails, axis=0).astype(BF16)
        for c in range(KIDS):
            row = pbc_ref[c, pl.ds(5 + len_ref[c] + k, 1), :]
            bc_out_ref[c, k] = jnp.concatenate([row[:, :W], row[:, W:]], axis=0).astype(BF16)
    send(x_out_ref, x_to_ref, sems.at[2])
    send(bc_out_ref, bc_to_ref, sems.at[3])
    for g in range(2):
        for c in range(KIDS):
            for q in range(4 * g, 4 * g + 4):
                b = (b0_ref, b1_ref)[c][:, N * g : N * (g + 1)]
                fresh = dot(xw_ref[c, :, chunks[q]], b, ((0,), (0,)))
                for j in range(4):
                    rows_at = slice(W * q + 64 * j, W * q + 64 * (j + 1))
                    h = 4 * q + j
                    new_ref[c, rows_at, :] = (
                        last_ref[c, h : h + 1, :] * messages[c][rows_at, :].astype(F32)
                        + fresh[64 * j : 64 * (j + 1)]
                    ).astype(BF16)
            half = pl.ds(GC * g, GC)
            send(new_ref.at[c, half], new_to_ref.at[c, half], new_sems.at[c, g])
    for copy in puts:
        copy.wait()


def shape(dims, kind):
    return jax.ShapeDtypeStruct(dims, kind)


def params(mib):
    return pltpu.CompilerParams(vmem_limit_bytes=mib * 2**20)


def cost(flops, moved, exps=0):
    return pl.CostEstimate(flops=flops, bytes_accessed=moved, transcendentals=exps)


def on_device(
    streams_in,
    beam_state_cache,
    conv_x_cache,
    conv_bc_cache,
    bc_inputs,
    unbiased_increments,
    parents,
    lengths,
    input_norm_gain,
    conv_x_weight,
    conv_bc_weight,
    a_log,
    dt_bias,
    skip_gain,
    out_gain,
):
    tens = lax.axis_size("tensor")
    peers = lax.axis_size("beam")
    section = lax.axis_index("section").astype(jnp.int32)[None]
    longer = shape((CD + 64 + EXTRA, N), BF16)
    message = shape((CD + 64, N), BF16)
    fwd, bwd = pl.pallas_call(
        pick_kernel,
        out_shape=(longer, message),
        in_specs=[HBM] * 4,
        out_specs=(HBM, HBM),
        scratch_shapes=[
            pltpu.SMEM(parents.shape, jnp.int32),
            pltpu.VMEM((3, KIDS, CD), BF16),
            pltpu.VMEM((KIDS, 3, 2, 256), BF16),
            pltpu.VMEM((KIDS, CD, N), BF16),
            pltpu.VMEM((2, 64, N), BF16),
            pltpu.SemaphoreType.DMA((3 + KIDS * PARTS,)),
            pltpu.SemaphoreType.DMA((3, PARTS + 1)),
        ],
        compiler_params=params(BIG),
        name="pick",
    )(
        parents,
        jnp.transpose(conv_x_cache[0], (1, 0, 2)),
        conv_bc_cache[0],
        beam_state_cache[0].reshape(KIDS, CD, N),
    )
    part = pl.pallas_call(
        square_kernel,
        out_shape=shape((KIDS, T), F32),
        in_specs=[VMEM],
        out_specs=VMEM,
        compiler_params=params(4),
        name="square",
    )(streams_in)

    def along(value, axis, steps):
        size = lax.axis_size(axis)
        return lax.ppermute(value, axis, [(i, (i + steps) % size) for i in range(size)])

    messages = (along(fwd, "beam", 1), along(bwd, "beam", -1))
    r1, r2, r3 = [along(part, "tensor", k) for k in range(1, tens)]

    bc = bc_inputs[0].reshape(KIDS, T, 512)
    inc = jnp.transpose(unbiased_increments[0], (0, 2, 1))
    skip = jnp.repeat(skip_gain, 64, axis=1)
    taps_bc = conv_bc_weight[0]
    taps = conv_x_weight[0]
    *decays, grow, weight, last = pl.pallas_call(
        pre_kernel,
        out_shape=(
            shape((T, CD), F32),
            shape((T, CD), F32),
            shape((KIDS, T, N), F32),
            shape((KIDS, T, N), F32),
            shape((KIDS, HD, N), F32),
        ),
        in_specs=[SMEM] + [VMEM] * 3,
        out_specs=tuple([VMEM] * 5),
        compiler_params=params(10),
        cost_estimate=cost(200_000_000, 5_000_000, 1_000_000),
        name="pre",
    )(lengths, inc, a_log, dt_bias)

    totals = pl.pallas_call(
        totals_kernel,
        out_shape=shape((KIDS, T), F32),
        in_specs=[VMEM] * 4,
        out_specs=VMEM,
        compiler_params=params(4),
        name="totals",
    )(part, r1, r2, r3)

    early = ()
    kept = {}
    for c in (1 - LATE, LATE):
        out_dims = ((KIDS, T, CD), (KIDS, T)) if c == LATE else ((T, CD), (1, T))
        result = pl.pallas_call(
            functools.partial(mid_kernel, c),
            out_shape=(
                shape(out_dims[0], BF16),
                shape(out_dims[1], F32),
                shape((T, CD), BF16),
                shape((T, CD), BF16),
                shape((T, 256), BF16),
            ),
            in_specs=[SMEM] * 2 + [VMEM] * (11 + len(early)),
            out_specs=tuple([VMEM] * 5),
            scratch_shapes=[
                pltpu.VMEM((72, 512), F32),
                pltpu.VMEM((8, CD), F32),
                pltpu.VMEM((T, CD), F32),
            ],
            compiler_params=params(12),
            cost_estimate=cost(1, 1),
            name="mid%d" % c,
        )(
            section,
            lengths,
            messages[c],
            bc,
            taps_bc,
            streams_in,
            totals,
            input_norm_gain,
            taps,
            skip,
            out_gain,
            decays[c],
            grow,
            *early,
        )
        early = result[:2]
        kept[c] = result[2:]
    mid, mid_part = early
    mixes, reads, b_mats = zip(kept[0], kept[1])

    moved = lax.ppermute(mid, "section", [(0, 1), (1, 0)])
    q1, q2, q3 = [
        lax.ppermute(
            mid_part,
            ("section", "tensor"),
            [(c * tens + i, (1 - c) * tens + (i + k) % tens) for c in range(2) for i in range(tens)],
        )
        for k in range(1, tens)
    ]

    others = pl.pallas_call(
        others_kernel,
        out_shape=shape((KIDS, T), F32),
        in_specs=[VMEM] * 3,
        out_specs=VMEM,
        compiler_params=params(4),
        cost_estimate=cost(10_000_000_000, 100_000_000, 0),
        name="others",
    )(q1, q2, q3)

    out, new, x_out, bc_out = pl.pallas_call(
        last_kernel,
        out_shape=(
            shape((KIDS, T, CD), BF16),
            shape((KIDS, CD, N), BF16),
            shape((3, KIDS, CD), BF16),
            shape((KIDS, 3, 2, W), BF16),
        ),
        in_specs=[SMEM] + [VMEM] * 17,
        out_specs=(HBM, HBM, HBM, HBM),
        scratch_shapes=[
            pltpu.VMEM((KIDS, 72, CD), F32),
            pltpu.VMEM((KIDS, T, CD), F32),
            pltpu.VMEM((KIDS, T, CD), BF16),
            pltpu.VMEM((KIDS, 72, 512), F32),
            pltpu.VMEM((KIDS, T, CD), BF16),
            pltpu.VMEM((KIDS, CD, N), BF16),
            pltpu.VMEM((3, KIDS, CD), BF16),
            pltpu.VMEM((KIDS, 3, 2, W), BF16),
            pltpu.SemaphoreType.DMA((6,)),
            pltpu.SemaphoreType.DMA((KIDS, 2)),
        ],
        compiler_params=params(14),
        cost_estimate=cost(200_000_000, 5_000_000, 1_000_000),
        name="last",
    )(
        lengths,
        others,
        input_norm_gain,
        taps,
        skip,
        out_gain,
        bc,
        *b_mats,
        last,
        moved,
        weight,
        *mixes,
        *reads,
        *messages,
    )
    return (
        out[None],
        new.reshape(1, KIDS, HD, 64, N),
        jnp.transpose(x_out, (1, 0, 2))[None],
        bc_out[None],
    )


def solution(mesh):
    placed = (
        P("beam", None, "tensor"),
        P("section", "beam", "tensor", None, None),
        P("section", "beam", None, "tensor"),
        P("section", "beam", None, None, "tensor"),
        P("section", "beam", None, None, "tensor"),
        P("section", "beam", None, "tensor"),
        P(),
        P("beam"),
        P("section", "tensor"),
        P("section", None, "tensor"),
        P("section", None, None, "tensor"),
        P("section", "tensor"),
        P("section", "tensor"),
        P("section", "tensor"),
        P("section", "tensor"),
    )
    return jax.shard_map(
        on_device,
        mesh=mesh,
        in_specs=placed,
        out_specs=(
            P("section", "beam", None, "tensor"),
            P("section", "beam", "tensor", None, None),
            P("section", "beam", None, "tensor"),
            P("section", "beam", None, None, "tensor"),
        ),
        check_vma=False,
    )
```
